32 devices in a mesh: ctx: 16 (over z, x, core), head: 2 (over y).
Axes of the slice: x: 2, y: 2, z: 4, core: 2. Of those that a mesh axis runs over, the one named last changes fastest.
Arguments:
- queries: bfloat16 [2048, 1024], P('ctx', 'head'), may hold values from -80 to 80
- keys: bfloat16 [2048, 256], P('ctx', 'head'), may hold values from -80 to 80
- values: bfloat16 [2048, 256], P('ctx', 'head'), may hold values from -6 to 6
- feat_q: bfloat16 [8, 128, 64], P('head'), may hold values from -1 to 1
- feat_k: bfloat16 [8, 128, 64], P('head'), may hold values from -1 to 1
Outputs:
- student: bfloat16 [2048, 1024], P('ctx', 'head')
- grad_q: float32 [8, 128, 64], P('head')
- grad_k: float32 [8, 128, 64], P('head')
- mean_error: float32 [], replicated
The draws below stay inside these ranges and needn't reach their ends.
All inputs are finite; a program needn't handle non-finite values.
Results may differ from the reference program's by a relative error of at most 0.007.
The reference program's roundings to bfloat16 on the way count: a program that leaves them out, or rounds other values in their place, can miss the bound.
Values may be sent and summed in bfloat16 or wider, within the bound.
A program may use at most 128 MiB of HBM per device.

```python
import jax
import jax.numpy as jnp
from jax import lax

HD = 128
FEAT = 64
TOK_DEV = 128
KV_HEADS = 2
HEADS = 8
SEQ = 2048


def drawn_pair(key):
    base_k = jax.random.normal(jax.random.fold_in(key, 1), (SEQ, KV_HEADS, HD), jnp.float32)
    base_q = jax.random.normal(jax.random.fold_in(key, 2), (SEQ, HEADS, HD), jnp.float32)
    base_q = jnp.clip(base_q, -80.0, 80.0)
    base_k = jnp.clip(base_k, -80.0, 80.0)
    return (base_q.reshape(SEQ, HEADS * HD), base_k.reshape(SEQ, KV_HEADS * HD))


def draw_queries(key, part):
    return drawn_pair(key)[0].astype(jnp.bfloat16)


def draw_keys(key, part):
    return drawn_pair(key)[1].astype(jnp.bfloat16)


def shard_levels(key, dims, pieces, low, largest):
    loudness = 1.0
    for position, shards_of in pieces:
        draws = jax.random.uniform(jax.random.fold_in(jax.random.fold_in(key, 6), position), (shards_of,), jnp.float32, low / len(pieces), largest / len(pieces))
        loudness = loudness * jnp.repeat(jnp.exp(draws), dims[position] // shards_of).reshape((-1,) + (1,) * (len(dims) - 1 - position))
    return loudness


def normal_values(key, shape, spread, most, pieces=(), kind=jnp.bfloat16):
    gain = shard_levels(key, shape, pieces, -0.22, 0.18) if pieces else 1.0
    result = jax.random.normal(key, shape, jnp.float32) * spread * gain
    return jnp.minimum(jnp.maximum(result, -most), most).astype(kind)


def setup_inputs(seed: int = 0) -> dict:
    arg_keys = jax.random.split(jax.random.key(seed), 6)
    queries = draw_queries(jax.random.fold_in(arg_keys[5], 71), 0)
    keys = draw_keys(jax.random.fold_in(arg_keys[5], 71), 0)
    values = normal_values(arg_keys[2], (SEQ, KV_HEADS * HD), 1.0, 6.0, ((0, 16), (1, 2)))
    feat_q = normal_values(arg_keys[3], (HEADS, HD, FEAT), (HD // 4) ** -0.5, 1.0, ((0, 2),))
    feat_k = normal_values(arg_keys[4], (HEADS, HD, FEAT), (HD // 4) ** -0.5, 1.0, ((0, 2),))
    return {"queries": queries, "keys": keys, "values": values, "feat_q": feat_q, "feat_k": feat_k}


precise_scores = lax.Precision.HIGHEST

def rounded_weights(array):
    return lax.optimization_barrier(array.astype(jnp.bfloat16)).astype(jnp.float32)

def feature_map(inputs, weight):
    logits = jnp.einsum('nhd,hdf->nhf', inputs, weight, precision=precise_scores)
    positive = jax.nn.softmax(logits, axis=-1)
    negative = jax.nn.softmax(-logits, axis=-1)
    return (positive, negative, rounded_weights(jnp.concatenate([positive, negative], axis=-1)))

def feature_grad(positive, negative, upstream):
    width = positive.shape[-1]
    up_pos = upstream[..., :width]
    up_neg = upstream[..., width:]
    return positive * (up_pos - lax.optimization_barrier(jnp.sum(up_pos * positive, axis=-1, keepdims=True))) - negative * (up_neg - lax.optimization_barrier(jnp.sum(up_neg * negative, axis=-1, keepdims=True)))

def reference(queries, keys, values, feat_q, feat_k):
    seq_len = queries.shape[0]
    head_count = feat_q.shape[0]
    head_dim = feat_q.shape[1]
    group_size = head_count // KV_HEADS
    block_length = TOK_DEV
    block_count = seq_len // block_length

    def spread_heads(array):
        widened = jnp.repeat(array.astype(jnp.float32).reshape(seq_len, KV_HEADS, head_dim), group_size, axis=1)
        return widened.reshape(block_count, block_length, head_count, head_dim)
    query_blocks = queries.astype(jnp.float32).reshape(block_count, block_length, head_count, head_dim)
    key_block_list = spread_heads(keys)
    value_block_list = spread_heads(values)
    weight_q = feat_q.astype(jnp.float32)
    weight_k = feat_k.astype(jnp.float32)
    logit_scale = head_dim ** (-0.5)
    block_offsets = jnp.arange(block_length, dtype=jnp.int32)

    def teacher_block(block_id):
        current_query = query_blocks[block_id]
        query_pos = block_id * block_length + block_offsets

        def absorb_block(key_index, partial_value_sum):
            running, totals, accumulated_output = partial_value_sum
            score_matrix = jnp.einsum('jlx,ulx->jlu', current_query, key_block_list[key_index], precision=precise_scores) * logit_scale
            key_positions = key_index * block_length + block_offsets
            allowed = (query_pos[:, None] >= key_positions[None, :])[:, None, :]
            score_matrix = jnp.where(allowed, score_matrix, -1e+30)
            new_max = jnp.maximum(running, lax.optimization_barrier(jnp.max(score_matrix, axis=-1)))
            attention_weights = jnp.where(allowed, jnp.exp(score_matrix - new_max[..., None]), 0.0)
            rescale_factor = jnp.exp(running - new_max)
            totals = totals * rescale_factor + lax.optimization_barrier(jnp.sum(attention_weights, axis=-1))
            accumulated_output = accumulated_output * rescale_factor[..., None] + jnp.einsum('uja,ajt->ujt', rounded_weights(attention_weights), value_block_list[key_index], precision=precise_scores)
            return (new_max, totals, accumulated_output)
        initial = (jnp.full((block_length, head_count), -1e+30, jnp.float32), jnp.zeros((block_length, head_count), jnp.float32), jnp.zeros((block_length, head_count, head_dim), jnp.float32))
        running, totals, accumulated_output = lax.fori_loop(0, block_id + 1, absorb_block, initial)
        return accumulated_output / totals[..., None]
    teacher = lax.map(teacher_block, jnp.arange(block_count, dtype=jnp.int32))
    causal = block_offsets[:, None] >= block_offsets[None, :]
    fdim2 = 2 * weight_q.shape[2]

    def forward(partial_value_sum, inputs):
        state, norm, grad_query, error = partial_value_sum
        current_query, key_now, value_now, teacher_now = inputs
        pos_q, neg_q, feat_query = feature_map(current_query, weight_q)
        pos_k, neg_k, feat_key = feature_map(key_now, weight_k)
        amat = jnp.einsum('ihf,jhf->hij', feat_query, feat_key, precision=precise_scores)
        amat = jnp.where(causal[None], amat, 0.0)
        numer = jnp.einsum('hij,jhd->ihd', rounded_weights(amat), value_now, precision=precise_scores) + jnp.einsum('ihf,hfd->ihd', feat_query, state, precision=precise_scores)
        denom = lax.optimization_barrier(jnp.sum(amat, axis=-1)).T + jnp.einsum('ihf,hf->ih', feat_query, norm, precision=precise_scores)
        output = numer / denom[..., None]
        diff = output - teacher_now
        error = error + jnp.sum(diff * diff)
        grad_out = 2.0 * diff
        grad_numer = grad_out / denom[..., None]
        grad_denom = -lax.optimization_barrier(jnp.sum(grad_out * output, axis=-1)) / denom
        numer_bf = rounded_weights(grad_numer)
        grad_mat = jnp.einsum('ihd,jhd->hij', numer_bf, value_now, precision=precise_scores) + grad_denom.T[:, :, None]
        grad_mat = rounded_weights(jnp.where(causal[None], grad_mat, 0.0))
        grad_fq = jnp.einsum('hij,jhf->ihf', grad_mat, feat_key, precision=precise_scores) + jnp.einsum('ihd,hfd->ihf', grad_numer, state, precision=precise_scores) + grad_denom[..., None] * norm[None]
        grad_logit = rounded_weights(feature_grad(pos_q, neg_q, grad_fq))
        grad_query = grad_query + jnp.einsum('bhd,bhf->hdf', current_query, grad_logit, precision=precise_scores)
        local_fk = jnp.einsum('hij,ihf->jhf', grad_mat, feat_query, precision=precise_scores)
        local_state = jnp.einsum('ihf,ihd->hfd', feat_query, numer_bf, precision=precise_scores)
        local_norm = jnp.einsum('ihf,ih->hf', feat_query, grad_denom, precision=precise_scores)
        state = state + jnp.einsum('jhf,jhd->hfd', feat_key, value_now, precision=precise_scores)
        norm = norm + lax.optimization_barrier(jnp.sum(feat_key, axis=0))
        return ((state, norm, grad_query, error), (output.astype(jnp.bfloat16), local_fk, local_state, local_norm))
    start_fwd = (jnp.zeros((head_count, fdim2, head_dim), jnp.float32), jnp.zeros((head_count, fdim2), jnp.float32), jnp.zeros(weight_q.shape, jnp.float32), jnp.zeros((), jnp.float32))
    finals, stacked = lax.scan(forward, start_fwd, (query_blocks, key_block_list, value_block_list, teacher))
    grad_query = finals[2]
    error = finals[3]
    outputs, local_fks, local_states, local_norms = stacked

    def backward(partial_value_sum, inputs):
        later_state, later_norm, grad_key = partial_value_sum
        key_now, value_now, local_fk, local_state, local_norm = inputs
        pos_k, neg_k, feat_key = feature_map(key_now, weight_k)
        grad_fk = local_fk + jnp.einsum('hfd,jhd->jhf', later_state, value_now, precision=precise_scores) + later_norm[None]
        grad_logit = rounded_weights(feature_grad(pos_k, neg_k, grad_fk))
        grad_key = grad_key + jnp.einsum('jhd,jhf->hdf', key_now, grad_logit, precision=precise_scores)
        return ((later_state + local_state, later_norm + local_norm, grad_key), None)
    start_back = (jnp.zeros((head_count, fdim2, head_dim), jnp.float32), jnp.zeros((head_count, fdim2), jnp.float32), jnp.zeros(weight_k.shape, jnp.float32))
    back_final, unused = lax.scan(backward, start_back, (key_block_list, value_block_list, local_fks, local_states, local_norms), reverse=True)
    student = outputs.reshape(seq_len, head_count * head_dim)
    mean_error = error / (seq_len * head_count * head_dim)
    return (student, grad_query, back_final[2], mean_error)
```

```python
import functools
import math

import jax
import jax.numpy as jnp
from jax import lax
from jax.experimental import pallas as pl
from jax.experimental.pallas import tpu as pltpu
from jax.sharding import PartitionSpec as P

MESH = pl.DeviceIdType.MESH
F32 = jnp.float32
BF16 = jnp.bfloat16
PLANE = 4


def dot(a, b):
    return lax.dot_general(a, b, (((1,), (0,)), ((), ())), preferred_element_type=F32)


def dot_nt(a, b):
    return lax.dot_general(a, b, (((1,), (1,)), ((), ())), preferred_element_type=F32)


def feature_map(logits):
    high = jnp.max(logits, axis=0, keepdims=True)
    low = jnp.min(logits, axis=0, keepdims=True)
    pos = jnp.exp(logits - high)
    neg = jnp.exp(low - logits)
    pos = pos * (1.0 / jnp.sum(pos, axis=0, keepdims=True))
    neg = neg * (1.0 / jnp.sum(neg, axis=0, keepdims=True))
    return jnp.concatenate([pos, neg], axis=0)


def feature_grad(both, upstream):
    width = both.shape[0] // 2
    pos, neg = both[:width], both[width:]
    up_pos, up_neg = upstream[:width], upstream[width:]
    return pos * (up_pos - jnp.sum(up_pos * pos, axis=0, keepdims=True)) - neg * (
        up_neg - jnp.sum(up_neg * neg, axis=0, keepdims=True)
    )


def split(array):
    high = array.astype(BF16)
    return high, (array - high.astype(F32)).astype(BF16)


def kernel(
    dims,
    q_ref, k_ref, v_ref, fq_ref, fk_ref,
    student_ref, gq_ref, gk_ref, err_ref,
    kv, wk, qs, top, total, acc, s_t, s_n, fqp, fkp, dfq, ldfk,
    st_out, st_in, st_fin, st_res, gq_out, gq_in, gk_out, gk_in, g_fin, g_res, e_out, e_in,
    z_send, x_send, c_send, kv_recv, a_send, a_recv, b_send, b_recv,
    q_send, q_recv, k_send, k_recv, g_send, g_recv, e_send, e_recv,
):
    n, heads_axis, rows, heads, hd, feat, state_pieces, grad_pieces = dims
    me = lax.axis_index("ctx")
    my_head = lax.axis_index("head")
    feat2 = 2 * feat
    place = me % PLANE
    level = me // PLANE
    levels = n // PLANE
    core_mate = me + 1 - 2 * (me % 2)
    x_mate = me + 2 - 4 * ((me // 2) % 2)
    span = PLANE * rows

    def copy(src, dst, send, recv, target):
        return pltpu.make_async_remote_copy(
            src_ref=src, dst_ref=dst, send_sem=send, recv_sem=recv,
            device_id=(target, my_head), device_id_type=MESH,
        )

    def peers(body):
        def step(k, carry):
            body((me + k) % n)
            return carry

        lax.fori_loop(1, n, step, 0)

    def guarded(index, pieces, body):
        if pieces == n:
            body()
        else:
            pl.when(index < pieces)(body)

    def head_mates(body):
        def step(k, carry):
            body((my_head + k) % heads_axis)
            return carry

        lax.fori_loop(1, heads_axis, step, 0)

    barrier = pltpu.get_barrier_semaphore()
    peers(lambda p: pl.semaphore_signal(barrier, inc=1, device_id=(p, my_head), device_id_type=MESH))
    head_mates(lambda p: pl.semaphore_signal(barrier, inc=1, device_id=(me, p), device_id_type=MESH))
    kv[me, 0] = k_ref[...]
    v_t = v_ref[...].astype(F32).T.astype(BF16)
    kv[me, 1] = v_t
    pl.semaphore_wait(barrier, n - 1 + heads_axis - 1)

    def z_copy(up):
        return copy(kv.at[me], kv.at[me], z_send.at[up], kv_recv.at[me], up * PLANE + place)

    def kv_copy(block, send, target):
        return copy(kv.at[block], kv.at[block], send, kv_recv.at[block], target)

    def x_copy(h):
        return kv_copy(h * PLANE + place, x_send.at[h], x_mate)

    def c_copy(h):
        return kv_copy(h * PLANE + place, c_send.at[0, h], core_mate)

    def f_copy(h):
        return kv_copy(h * PLANE + x_mate % PLANE, c_send.at[1, h], core_mate)

    def kv_wait(block):
        kv_copy(block, z_send.at[0], core_mate).wait_recv()

    def loop(low, high, body):
        def step(i, carry):
            body(i)
            return carry

        lax.fori_loop(low, high, step, 0)

    x_copy(level).start()
    c_copy(level).start()
    loop(level + 1, levels, lambda up: z_copy(up).start())

    def weight_rows(ref):
        return jnp.concatenate(
            [ref[g].astype(F32).T.astype(BF16) for g in range(heads)], axis=0
        )

    w_k = weight_rows(fk_ref)
    wk[...] = w_k
    w_q = weight_rows(fq_ref)
    own_k = dot_nt(w_k, k_ref[...])
    for g in range(heads):
        q_g = q_ref[:, g * hd : (g + 1) * hd]
        qs[g * rows : (g + 1) * rows, :] = q_g
        fqp[g] = feature_map(dot_nt(w_q[g * feat : (g + 1) * feat], q_g))
        fkp[g] = feature_map(own_k[g * feat : (g + 1) * feat])
    top[...] = jnp.full_like(top, -1e30)
    total[...] = jnp.zeros_like(total)
    acc[...] = jnp.zeros_like(acc)
    s_t[...] = jnp.zeros_like(s_t)
    s_n[...] = jnp.zeros_like(s_n)

    def relay(t):
        h = level - 1 - t
        kv_wait(h * PLANE + place)
        x_copy(h).start()
        c_copy(h).start()

    loop(0, level, relay)

    def pass_on(t):
        h = level - t
        kv_wait(h * PLANE + x_mate % PLANE)
        f_copy(h).start()

    loop(0, level + 1, pass_on)

    scale = hd ** (-0.5) / math.log(2.0)
    ones = jnp.ones((hd, span), BF16)

    def absorb(t):
        h = level - t
        kv_wait(h * PLANE + core_mate % PLANE)
        kv_wait(h * PLANE + core_mate % PLANE + 2 - 4 * ((core_mate // 2) % 2))
        keys = kv[pl.ds(h * PLANE, PLANE), 0].reshape(span, hd)
        vals = jnp.concatenate([kv[h * PLANE + b, 1] for b in range(PLANE)], axis=1)
        key_pos = h * span + lax.broadcasted_iota(jnp.int32, (span, rows), 0)
        query_pos = me * rows + lax.broadcasted_iota(jnp.int32, (span, rows), 1)
        allowed = key_pos <= query_pos
        for g in range(heads):
            scores = dot_nt(keys, qs[g * rows : (g + 1) * rows, :])
            scores = jnp.where(allowed, scores, -1e30)
            old = top[g]
            new = jnp.maximum(old, jnp.max(scores, axis=0, keepdims=True))
            top[g] = new
            shrink = jnp.exp2((old - new) * scale)
            weights = jnp.exp2((scores - new) * scale)
            total[g] = total[g] * shrink + jnp.sum(weights, axis=0, keepdims=True)
            acc[g] = acc[g] * shrink + dot(vals, weights.astype(BF16))
        logits = dot_nt(wk[...], keys)
        before = h * span + lax.broadcasted_iota(jnp.int32, (feat2, span), 1) < me * rows
        maps = jnp.concatenate(
            [
                jnp.where(before, feature_map(logits[g * feat : (g + 1) * feat]), 0.0).astype(BF16)
                for g in range(heads)
            ],
            axis=0,
        )
        wide = jnp.concatenate([vals, ones], axis=0)
        s_t[...] += dot_nt(wide, maps)
        s_n[...] += dot_nt(maps, wide)

    loop(0, level + 1, absorb)

    key_row = lax.broadcasted_iota(jnp.int32, (rows, rows), 0)
    query_col = lax.broadcasted_iota(jnp.int32, (rows, rows), 1)
    causal = key_row <= query_col
    per_head = state_pieces // heads
    piece = heads * feat2 // state_pieces
    squares = jnp.zeros((hd, rows), F32)
    norm_rows = []
    values = v_ref[...]
    for g in range(heads):
        fq_t = fqp[g].astype(BF16)
        fk_t = fkp[g].astype(BF16)
        fk_n = fkp[g].T.astype(BF16)
        amat = jnp.where(causal, dot(fk_n, fq_t), 0.0)
        high, low = split(s_t[:, g * feat2 : (g + 1) * feat2])
        prior = dot(jnp.concatenate([high, low], axis=1), jnp.concatenate([fq_t, fq_t], axis=0))
        numer = dot(v_t, amat.astype(BF16)) + prior[:hd]
        denom = jnp.sum(amat, axis=0, keepdims=True) + prior[hd : hd + 1]
        inverse = 1.0 / denom
        y = numer * inverse
        student_ref[:, g * hd : (g + 1) * hd] = y.T.astype(BF16)
        diff = y - acc[g] * (1.0 / total[g])
        squares = squares + diff * diff
        dy = 2.0 * diff
        dnumer = dy * inverse
        dden = -jnp.sum(dy * y, axis=0, keepdims=True) * inverse
        dnb = dnumer.astype(BF16)
        dmat = jnp.where(causal, dot(values, dnb) + dden, 0.0).astype(BF16)
        state = dot_nt(fq_t, dnb).astype(BF16)
        st_out[g * per_head : (g + 1) * per_head, :piece, :] = state.reshape(per_head, piece, hd)
        d_high, d_low = split(jnp.broadcast_to(dden, (16, rows)))
        norm_rows.append(dot_nt(d_high, fq_t) + dot_nt(d_low, fq_t))
        high, low = split(s_n[g * feat2 : (g + 1) * feat2, :hd])
        dfq[g] = (
            dot(jnp.concatenate([fk_t, high, low], axis=1), jnp.concatenate([dmat, dnb, dnb], axis=0))
            + s_n[g * feat2 : (g + 1) * feat2, hd:] * dden
        )
        ldfk[g] = dot_nt(fq_t, dmat)
    error = jnp.sum(jnp.sum(squares, axis=0, keepdims=True), axis=1, keepdims=True)
    extra_row = lax.broadcasted_iota(jnp.int32, (16, hd), 0)

    def with_error(norms, value):
        first = value.astype(BF16).astype(F32)
        return jnp.where(
            extra_row < 8, norms, jnp.where(extra_row < 12, first, value - first)
        ).astype(BF16)

    error = jnp.broadcast_to(error, (16, hd))
    for g in range(heads):
        extra = with_error(norm_rows[g], error)
        for p in range(g * per_head, (g + 1) * per_head):
            st_out[p, piece:, :] = extra

    def a_copy(p, s):
        return copy(st_out.at[p], st_in.at[s], a_send.at[p], a_recv.at[s], p)

    peers(lambda p: guarded(p, state_pieces, lambda: a_copy(p, me).start()))

    grad_rows = heads * feat // grad_pieces
    grad_per_head = grad_pieces // heads
    for g in range(heads):
        dlq = feature_grad(fqp[g], dfq[g]).astype(BF16)
        part = dot(dlq, qs[g * rows : (g + 1) * rows, :]).astype(BF16)
        gq_out[g * grad_per_head : (g + 1) * grad_per_head] = part.reshape(
            grad_per_head, grad_rows, hd
        )

    def q_copy(p, s):
        return copy(gq_out.at[p], gq_in.at[s], q_send.at[p], q_recv.at[s], p)

    def b_copy(d, s):
        return copy(st_fin.at[d], st_res.at[s], b_send.at[d], b_recv.at[s], d)

    def reduce_states():
        st_in[me] = st_out[me]
        peers(lambda s: a_copy(0, s).wait_recv())
        extras = jnp.sum(st_in[:, piece:, :].astype(F32), axis=0)
        summed = jnp.sum(jnp.where(extra_row < 8, 0.0, extras), axis=0, keepdims=True) * 0.25
        summed = jnp.broadcast_to(summed, (16, hd))

        def suffix(t, carry):
            states, norms = carry
            d = n - 1 - t
            st_fin[d, :piece, :] = states.astype(BF16)
            st_fin[d, piece:, :] = with_error(norms, summed)
            return (
                states + st_in[d, :piece, :].astype(F32),
                norms + st_in[d, piece:, :].astype(F32),
            )

        lax.fori_loop(
            0, n, suffix, (jnp.zeros((piece, hd), F32), jnp.zeros((16, hd), F32))
        )
        peers(lambda d: b_copy(d, me).start())
        st_res[me] = st_fin[me]

    guarded(me, state_pieces, reduce_states)
    peers(lambda p: guarded(p, grad_pieces, lambda: q_copy(p, me).start()))
    peers(lambda s: guarded(s, state_pieces, lambda: b_copy(0, s).wait_recv()))

    last = st_res[0, piece:, :].astype(F32)
    e_out[...] = jnp.broadcast_to(
        jnp.sum(jnp.where(extra_row < 8, 0.0, last), axis=0, keepdims=True) * 0.25, e_out.shape
    )

    def e_copy(p, s):
        return pltpu.make_async_remote_copy(
            src_ref=e_out, dst_ref=e_in.at[s], send_sem=e_send.at[p], recv_sem=e_recv.at[s],
            device_id=(me, p), device_id_type=MESH,
        )

    for g in range(heads):
        later = st_res[g * per_head : (g + 1) * per_head, :piece, :].reshape(feat2, hd)
        norm = jnp.broadcast_to(
            st_res[g * per_head, piece : piece + 16, :].astype(F32)[:1], (rows, feat2)
        ).T
        dfk = ldfk[g] + dot(later, v_t) + norm
        dlk = feature_grad(fkp[g], dfk).astype(BF16)
        part = dot(dlk, k_ref[...]).astype(BF16)
        gk_out[g * grad_per_head : (g + 1) * grad_per_head] = part.reshape(
            grad_per_head, grad_rows, hd
        )

    def k_copy(p, s):
        return copy(gk_out.at[p], gk_in.at[s], k_send.at[p], k_recv.at[s], p)

    def g_copy(d, s):
        return copy(g_fin, g_res.at[s], g_send.at[d], g_recv.at[s], d)

    peers(lambda p: guarded(p, grad_pieces, lambda: k_copy(p, me).start()))
    head_mates(lambda p: e_copy(p, my_head).start())

    def reduce_grads():
        gq_in[me] = gq_out[me]
        gk_in[me] = gk_out[me]
        peers(lambda s: q_copy(0, s).wait_recv())
        g_fin[:grad_rows] = jnp.sum(gq_in[...].astype(F32), axis=0).astype(BF16)
        peers(lambda s: k_copy(0, s).wait_recv())
        g_fin[grad_rows:] = jnp.sum(gk_in[...].astype(F32), axis=0).astype(BF16)
        peers(lambda d: g_copy(d, me).start())
        g_res[me] = g_fin[...]

    guarded(me, grad_pieces, reduce_grads)

    e_in[my_head] = e_out[...]
    head_mates(lambda s: e_copy(0, s).wait_recv())
    entries = n * rows * heads * heads_axis * hd
    err_ref[...] = jnp.sum(e_in[...], axis=0) / entries
    head_mates(lambda p: e_copy(p, my_head).wait_send())
    x_copy(level).wait_send()
    c_copy(level).wait_send()
    loop(level + 1, levels, lambda up: z_copy(up).wait_send())

    def relay_end(t):
        x_copy(t).wait_send()
        c_copy(t).wait_send()

    loop(0, level, relay_end)
    loop(0, level + 1, lambda t: f_copy(t).wait_send())
    peers(lambda p: guarded(p, state_pieces, lambda: a_copy(p, me).wait_send()))
    guarded(me, state_pieces, lambda: peers(lambda d: b_copy(d, me).wait_send()))
    peers(lambda p: guarded(p, grad_pieces, lambda: q_copy(p, me).wait_send()))
    peers(lambda p: guarded(p, grad_pieces, lambda: k_copy(p, me).wait_send()))
    peers(lambda s: guarded(s, grad_pieces, lambda: g_copy(0, s).wait_recv()))
    for g in range(heads):
        both = g_res[g * grad_per_head : (g + 1) * grad_per_head].astype(F32)
        gq_ref[g] = both[:, :grad_rows].reshape(feat, hd).T
        gk_ref[g] = both[:, grad_rows:].reshape(feat, hd).T
    guarded(me, grad_pieces, lambda: peers(lambda d: g_copy(d, me).wait_send()))


def on_device(queries, keys, values, feat_q, feat_k):
    rows, hd = keys.shape
    heads, _, feat = feat_q.shape
    n = lax.axis_size("ctx")
    heads_axis = lax.axis_size("head")
    feat2 = 2 * feat
    state_pieces = min(n, heads * feat2 // 16)
    grad_pieces = min(n, heads * feat // 16)
    dims = (n, heads_axis, rows, heads, hd, feat, state_pieces, grad_pieces)
    piece = heads * feat2 // state_pieces + 16
    grad_rows = heads * feat // grad_pieces
    levels = n // PLANE
    dma = pltpu.SemaphoreType.DMA
    vmem = pl.BlockSpec(memory_space=pltpu.VMEM)
    student, grad_q, grad_k, error = pl.pallas_call(
        functools.partial(kernel, dims),
        out_shape=(
            jax.ShapeDtypeStruct((rows, heads * hd), BF16),
            jax.ShapeDtypeStruct((heads, hd, feat), F32),
            jax.ShapeDtypeStruct((heads, hd, feat), F32),
            jax.ShapeDtypeStruct((8, hd), F32),
        ),
        in_specs=[vmem] * 5,
        out_specs=(vmem,) * 4,
        scratch_shapes=[
            pltpu.VMEM((n, 2, rows, hd), BF16),
            pltpu.VMEM((heads * feat, hd), BF16),
            pltpu.VMEM((heads * rows, hd), BF16),
            pltpu.VMEM((heads, 1, rows), F32),
            pltpu.VMEM((heads, 1, rows), F32),
            pltpu.VMEM((heads, hd, rows), F32),
            pltpu.VMEM((2 * hd, heads * feat2), F32),
            pltpu.VMEM((heads * feat2, 2 * hd), F32),
            pltpu.VMEM((heads, feat2, rows), F32),
            pltpu.VMEM((heads, feat2, rows), F32),
            pltpu.VMEM((heads, feat2, rows), F32),
            pltpu.VMEM((heads, feat2, rows), F32),
            pltpu.VMEM((state_pieces, piece, hd), BF16),
            pltpu.VMEM((n, piece, hd), BF16),
            pltpu.VMEM((n, piece, hd), BF16),
            pltpu.VMEM((state_pieces, piece, hd), BF16),
            pltpu.VMEM((grad_pieces, grad_rows, hd), BF16),
            pltpu.VMEM((n, grad_rows, hd), BF16),
            pltpu.VMEM((grad_pieces, grad_rows, hd), BF16),
            pltpu.VMEM((n, grad_rows, hd), BF16),
            pltpu.VMEM((2 * grad_rows, hd), BF16),
            pltpu.VMEM((grad_pieces, 2 * grad_rows, hd), BF16),
            pltpu.VMEM((8, hd), F32),
            pltpu.VMEM((heads_axis, 8, hd), F32),
            dma((levels,)),
            dma((levels,)),
            dma((2, levels)),
            dma((n,)),
            dma((n,)),
            dma((n,)),
            dma((n,)),
            dma((n,)),
            dma((n,)),
            dma((n,)),
            dma((n,)),
            dma((n,)),
            dma((n,)),
            dma((n,)),
            dma((heads_axis,)),
            dma((heads_axis,)),
        ],
        compiler_params=pltpu.CompilerParams(
            collective_id=0, has_side_effects=True, vmem_limit_bytes=40 * 1024 * 1024
        ),
    )(queries, keys, values, feat_q, feat_k)
    return student, grad_q, grad_k, error[0, 0]


def solution(mesh):
    in_specs = (
        P("ctx", "head"),
        P("ctx", "head"),
        P("ctx", "head"),
        P("head", None, None),
        P("head", None, None),
    )
    out_specs = (P("ctx", "head"), P("head", None, None), P("head", None, None), P())
    return jax.shard_map(
        on_device, mesh=mesh, in_specs=in_specs, out_specs=out_specs, check_vma=False
    )
```

```python
import functools
import math

import jax
import jax.numpy as jnp
from jax import lax
from jax.experimental import pallas as pl
from jax.experimental.pallas import tpu as pltpu
from jax.sharding import PartitionSpec as P

MESH = pl.DeviceIdType.MESH
F32 = jnp.float32
BF16 = jnp.bfloat16
PLANE = 4


def dot(a, b):
    return lax.dot_general(a, b, (((1,), (0,)), ((), ())), preferred_element_type=F32)


def dot_nt(a, b):
    return lax.dot_general(a, b, (((1,), (1,)), ((), ())), preferred_element_type=F32)


def feature_map(logits):
    high = jnp.max(logits, axis=0, keepdims=True)
    low = jnp.min(logits, axis=0, keepdims=True)
    pos = jnp.exp(logits - high)
    neg = jnp.exp(low - logits)
    pos = pos * (1.0 / jnp.sum(pos, axis=0, keepdims=True))
    neg = neg * (1.0 / jnp.sum(neg, axis=0, keepdims=True))
    return jnp.concatenate([pos, neg], axis=0)


def feature_grad(both, upstream):
    width = both.shape[0] // 2
    pos, neg = both[:width], both[width:]
    up_pos, up_neg = upstream[:width], upstream[width:]
    return pos * (up_pos - jnp.sum(up_pos * pos, axis=0, keepdims=True)) - neg * (
        up_neg - jnp.sum(up_neg * neg, axis=0, keepdims=True)
    )


def split(array):
    high = array.astype(BF16)
    return high, (array - high.astype(F32)).astype(BF16)


def kernel(
    dims,
    q_any, k_any, v_any, fq_any, fk_any,
    student_ref, gq_ref, gk_ref, err_ref,
    q_ref, v_ref, fq_ref, fk_ref, in_sem, numl, denl, x_out, x_in, n_send, n_recv,
    kv, qs, top, total, acc, s_t, s_n, fqp, fkp, dfq, ldfk,
    st_out, st_in, st_fin, st_res, gq_out, gq_in, gk_out, gk_in, g_fin, g_res, e_out, e_in,
    z_send, x_send, c_send, kv_recv, a_send, a_recv, b_send, b_recv,
    q_send, q_recv, k_send, k_recv, g_send, g_recv, e_send, e_recv,
):
    n, heads_axis, rows, heads, hd, feat, state_pieces, grad_pieces = dims
    me = lax.axis_index("ctx")
    my_head = lax.axis_index("head")
    feat2 = 2 * feat
    place = me % PLANE
    level = me // PLANE
    levels = n // PLANE
    core_mate = me + 1 - 2 * (me % 2)
    x_mate = me + 2 - 4 * ((me // 2) % 2)
    span = PLANE * rows

    def copy(src, dst, send, recv, target):
        return pltpu.make_async_remote_copy(
            src_ref=src, dst_ref=dst, send_sem=send, recv_sem=recv,
            device_id=(target, my_head), device_id_type=MESH,
        )

    def peers(body):
        def step(k, carry):
            body((me + k) % n)
            return carry

        lax.fori_loop(1, n, step, 0)

    def guarded(index, pieces, body):
        if pieces == n:
            body()
        else:
            pl.when(index < pieces)(body)

    def head_mates(body):
        def step(k, carry):
            body((my_head + k) % heads_axis)
            return carry

        lax.fori_loop(1, heads_axis, step, 0)

    loads = [
        pltpu.make_async_copy(src, dst, in_sem.at[i])
        for i, (src, dst) in enumerate(
            ((k_any, kv.at[me, 0]), (v_any, v_ref), (fk_any, fk_ref), (q_any, q_ref), (fq_any, fq_ref))
        )
    ]
    for load in loads:
        load.start()

    barrier = pltpu.get_barrier_semaphore()
    peers(lambda p: pl.semaphore_signal(barrier, inc=1, device_id=(p, my_head), device_id_type=MESH))
    head_mates(lambda p: pl.semaphore_signal(barrier, inc=1, device_id=(me, p), device_id_type=MESH))
    loads[0].wait()
    loads[1].wait()
    v_t = v_ref[...].astype(F32).T.astype(BF16)
    kv[me, 1] = v_t
    pl.semaphore_wait(barrier, n - 1 + heads_axis - 1)

    def z_copy(up):
        return copy(kv.at[me], kv.at[me], z_send.at[up], kv_recv.at[me], up * PLANE + place)

    def kv_copy(block, send, target):
        return copy(kv.at[block], kv.at[block], send, kv_recv.at[block], target)

    def x_copy(h):
        return kv_copy(h * PLANE + place, x_send.at[h], x_mate)

    def c_copy(h):
        return kv_copy(h * PLANE + place, c_send.at[0, h], core_mate)

    def f_copy(h):
        return kv_copy(h * PLANE + x_mate % PLANE, c_send.at[1, h], core_mate)

    def kv_wait(block):
        kv_copy(block, z_send.at[0], core_mate).wait_recv()

    def loop(low, high, body):
        def step(i, carry):
            body(i)
            return carry

        lax.fori_loop(low, high, step, 0)

    x_copy(level).start()
    c_copy(level).start()
    loop(level + 1, levels, lambda up: z_copy(up).start())

    key_row = lax.broadcasted_iota(jnp.int32, (rows, rows), 0)
    query_col = lax.broadcasted_iota(jnp.int32, (rows, rows), 1)
    causal = key_row <= query_col
    for load in loads[2:]:
        load.wait()
    w_k = fk_ref[...].reshape(heads * feat, hd)
    w_q = fq_ref[...].reshape(heads * feat, hd)
    own_k = dot_nt(w_k, kv[me, 0])
    for g in range(heads):
        q_g = q_ref[:, g * hd : (g + 1) * hd]
        qs[g * rows : (g + 1) * rows, :] = q_g
        map_q = feature_map(dot_nt(w_q[g * feat : (g + 1) * feat], q_g))
        map_k = feature_map(own_k[g * feat : (g + 1) * feat])
        fqp[g] = map_q
        fkp[g] = map_k
        amat = jnp.where(causal, dot(map_k.T.astype(BF16), map_q.astype(BF16)), 0.0)
        numl[g] = dot(v_t, amat.astype(BF16))
        denl[g] = jnp.sum(amat, axis=0, keepdims=True)
    top[...] = jnp.full_like(top, -1e30)
    total[...] = jnp.zeros_like(total)
    acc[...] = jnp.zeros_like(acc)
    s_t[...] = jnp.zeros_like(s_t)
    s_n[...] = jnp.zeros_like(s_n)

    def relay(h):
        kv_wait(h * PLANE + place)
        x_copy(h).start()
        c_copy(h).start()

    def pass_on(h):
        kv_wait(h * PLANE + x_mate % PLANE)
        f_copy(h).start()

    scale = hd ** (-0.5) / math.log(2.0)
    ones = jnp.ones((hd, span), BF16)

    def absorb(t):
        h = level - t
        kv_wait(h * PLANE + core_mate % PLANE)
        kv_wait(h * PLANE + core_mate % PLANE + 2 - 4 * ((core_mate // 2) % 2))
        keys = kv[pl.ds(h * PLANE, PLANE), 0].reshape(span, hd)
        vals = jnp.concatenate([kv[h * PLANE + b, 1] for b in range(PLANE)], axis=1)
        key_pos = h * span + lax.broadcasted_iota(jnp.int32, (span, rows), 0)
        query_pos = me * rows + lax.broadcasted_iota(jnp.int32, (span, rows), 1)
        allowed = key_pos <= query_pos
        for g in range(heads):
            scores = dot_nt(keys, qs[g * rows : (g + 1) * rows, :])
            scores = jnp.where(allowed, scores, -1e30)
            old = top[g]
            new = jnp.maximum(old, jnp.max(scores, axis=0, keepdims=True))
            top[g] = new
            shrink = jnp.exp2((old - new) * scale)
            weights = jnp.exp2((scores - new) * scale)
            total[g] = total[g] * shrink + jnp.sum(weights, axis=0, keepdims=True)
            acc[g] = acc[g] * shrink + dot(vals, weights.astype(BF16))
        logits = dot_nt(fk_ref[...].reshape(heads * feat, hd), keys)
        before = h * span + lax.broadcasted_iota(jnp.int32, (feat2, span), 1) < me * rows
        maps = jnp.concatenate(
            [
                jnp.where(before, feature_map(logits[g * feat : (g + 1) * feat]), 0.0).astype(BF16)
                for g in range(heads)
            ],
            axis=0,
        )
        wide = jnp.concatenate([vals, ones], axis=0)
        s_t[...] += dot_nt(wide, maps)
        s_n[...] += dot_nt(maps, wide)

    def pipeline(u):
        pl.when(u <= level + 1)(lambda: pass_on(level - (u - 1)))
        pl.when(u <= level)(lambda: relay(level - u))
        pl.when(u >= 2)(lambda: absorb(u - 2))

    loop(1, level + 3, pipeline)

    per_head = state_pieces // heads
    piece = heads * feat2 // state_pieces
    squares = jnp.zeros((hd, rows), F32)
    norm_rows = []
    values = v_ref[...]
    for g in range(heads):
        fq_t = fqp[g].astype(BF16)
        fk_t = fkp[g].astype(BF16)
        high, low = split(s_t[:, g * feat2 : (g + 1) * feat2])
        prior = dot(jnp.concatenate([high, low], axis=1), jnp.concatenate([fq_t, fq_t], axis=0))
        numer = numl[g] + prior[:hd]
        denom = denl[g] + prior[hd : hd + 1]
        inverse = 1.0 / denom
        y = numer * inverse
        student_ref[:, g * hd : (g + 1) * hd] = y.T.astype(BF16)
        diff = y - acc[g] * (1.0 / total[g])
        squares = squares + diff * diff
        dy = 2.0 * diff
        dnumer = dy * inverse
        dden = -jnp.sum(dy * y, axis=0, keepdims=True) * inverse
        dnb = dnumer.astype(BF16)
        dmat = jnp.where(causal, dot(values, dnb) + dden, 0.0).astype(BF16)
        state = dot_nt(fq_t, dnb).astype(BF16)
        st_out[g * per_head : (g + 1) * per_head] = state.reshape(per_head, piece, hd)
        d_high, d_low = split(jnp.broadcast_to(dden, (16, rows)))
        norm_rows.append(dot_nt(d_high, fq_t) + dot_nt(d_low, fq_t))
        high, low = split(s_n[g * feat2 : (g + 1) * feat2, :hd])
        dfq[g] = (
            dot(jnp.concatenate([fk_t, high, low], axis=1), jnp.concatenate([dmat, dnb, dnb], axis=0))
            + s_n[g * feat2 : (g + 1) * feat2, hd:] * dden
        )
        ldfk[g] = dot_nt(fq_t, dmat)
    error = jnp.sum(jnp.sum(squares, axis=0, keepdims=True), axis=1, keepdims=True)
    first = error.astype(BF16).astype(F32)
    extra_row = lax.broadcasted_iota(jnp.int32, (16, hd), 0)
    extra = jnp.where(extra_row < 12, first, error - first)
    for g in range(heads):
        extra = jnp.where(extra_row == g, norm_rows[g], extra)
    x_out[...] = extra.astype(BF16)

    def n_copy(p, s):
        return copy(x_out, x_in.at[s], n_send.at[p], n_recv.at[s], p)

    def a_copy(p, s):
        return copy(st_out.at[p], st_in.at[s], a_send.at[p], a_recv.at[s], p)

    peers(lambda p: guarded(p, state_pieces, lambda: a_copy(p, me).start()))
    peers(lambda p: n_copy(p, me).start())

    grad_rows = heads * feat // grad_pieces
    grad_per_head = grad_pieces // heads
    for g in range(heads):
        dlq = feature_grad(fqp[g], dfq[g]).astype(BF16)
        part = dot(dlq, qs[g * rows : (g + 1) * rows, :]).astype(BF16)
        gq_out[g * grad_per_head : (g + 1) * grad_per_head] = part.reshape(
            grad_per_head, grad_rows, hd
        )

    def q_copy(p, s):
        return copy(gq_out.at[p], gq_in.at[s], q_send.at[p], q_recv.at[s], p)

    def b_copy(d, s):
        return copy(st_fin.at[d], st_res.at[s], b_send.at[d], b_recv.at[s], d)

    def reduce_states():
        st_in[me] = st_out[me]
        peers(lambda s: a_copy(0, s).wait_recv())

        def suffix(t, states):
            d = n - 1 - t
            st_fin[d] = states.astype(BF16)
            return states + st_in[d].astype(F32)

        lax.fori_loop(0, n, suffix, jnp.zeros((piece, hd), F32))
        peers(lambda d: b_copy(d, me).start())
        st_res[me] = st_fin[me]

    guarded(me, state_pieces, reduce_states)
    peers(lambda p: guarded(p, grad_pieces, lambda: q_copy(p, me).start()))

    x_in[me] = x_out[...]
    peers(lambda s: n_copy(0, s).wait_recv())
    extras = x_in[...].astype(F32)
    later_norms = jnp.sum(
        jnp.where(lax.broadcasted_iota(jnp.int32, extras.shape, 0) > me, extras, 0.0), axis=0
    )
    summed = jnp.sum(jnp.where(extra_row < 8, 0.0, jnp.sum(extras, axis=0)), axis=0, keepdims=True)
    e_out[...] = jnp.broadcast_to(summed * 0.25, e_out.shape)

    def e_copy(p, s):
        return pltpu.make_async_remote_copy(
            src_ref=e_out, dst_ref=e_in.at[s], send_sem=e_send.at[p], recv_sem=e_recv.at[s],
            device_id=(me, p), device_id_type=MESH,
        )

    head_mates(lambda p: e_copy(p, my_head).start())
    for g in range(heads):
        norm = jnp.broadcast_to(later_norms[g : g + 1], (rows, feat2)).T
        ldfk[g] += norm

    peers(lambda s: guarded(s, state_pieces, lambda: b_copy(0, s).wait_recv()))
    for g in range(heads):
        later = st_res[g * per_head : (g + 1) * per_head].reshape(feat2, hd)
        dfk = ldfk[g] + dot(later, v_t)
        dlk = feature_grad(fkp[g], dfk).astype(BF16)
        part = dot(dlk, kv[me, 0]).astype(BF16)
        gk_out[g * grad_per_head : (g + 1) * grad_per_head] = part.reshape(
            grad_per_head, grad_rows, hd
        )

    def k_copy(p, s):
        return copy(gk_out.at[p], gk_in.at[s], k_send.at[p], k_recv.at[s], p)

    def g_copy(d, s):
        return copy(g_fin, g_res.at[s], g_send.at[d], g_recv.at[s], d)

    peers(lambda p: guarded(p, grad_pieces, lambda: k_copy(p, me).start()))

    def reduce_grads():
        gq_in[me] = gq_out[me]
        gk_in[me] = gk_out[me]
        peers(lambda s: q_copy(0, s).wait_recv())
        g_fin[:grad_rows] = jnp.sum(gq_in[...].astype(F32), axis=0).astype(BF16)
        peers(lambda s: k_copy(0, s).wait_recv())
        g_fin[grad_rows:] = jnp.sum(gk_in[...].astype(F32), axis=0).astype(BF16)
        peers(lambda d: g_copy(d, me).start())
        g_res[me] = g_fin[...]

    guarded(me, grad_pieces, reduce_grads)

    e_in[my_head] = e_out[...]
    head_mates(lambda s: e_copy(0, s).wait_recv())
    entries = n * rows * heads * heads_axis * hd
    err_ref[...] = jnp.sum(e_in[...], axis=0) / entries
    head_mates(lambda p: e_copy(p, my_head).wait_send())
    peers(lambda p: n_copy(p, me).wait_send())
    x_copy(level).wait_send()
    c_copy(level).wait_send()
    loop(level + 1, levels, lambda up: z_copy(up).wait_send())

    def relay_end(t):
        x_copy(t).wait_send()
        c_copy(t).wait_send()

    loop(0, level, relay_end)
    loop(0, level + 1, lambda t: f_copy(t).wait_send())
    peers(lambda p: guarded(p, state_pieces, lambda: a_copy(p, me).wait_send()))
    guarded(me, state_pieces, lambda: peers(lambda d: b_copy(d, me).wait_send()))
    peers(lambda p: guarded(p, grad_pieces, lambda: q_copy(p, me).wait_send()))
    peers(lambda p: guarded(p, grad_pieces, lambda: k_copy(p, me).wait_send()))
    peers(lambda s: guarded(s, grad_pieces, lambda: g_copy(0, s).wait_recv()))
    for g in range(heads):
        both = g_res[g * grad_per_head : (g + 1) * grad_per_head].astype(F32)
        gq_ref[g] = both[:, :grad_rows].reshape(feat, hd)
        gk_ref[g] = both[:, grad_rows:].reshape(feat, hd)
    guarded(me, grad_pieces, lambda: peers(lambda d: g_copy(d, me).wait_send()))


def on_device(queries, keys, values, feat_q, feat_k):
    rows, hd = keys.shape
    heads, _, feat = feat_q.shape
    n = lax.axis_size("ctx")
    heads_axis = lax.axis_size("head")
    feat2 = 2 * feat
    state_pieces = min(n, heads * feat2 // 16)
    grad_pieces = min(n, heads * feat // 16)
    dims = (n, heads_axis, rows, heads, hd, feat, state_pieces, grad_pieces)
    piece = heads * feat2 // state_pieces
    grad_rows = heads * feat // grad_pieces
    levels = n // PLANE
    dma = pltpu.SemaphoreType.DMA
    vmem = pl.BlockSpec(memory_space=pltpu.VMEM)
    student, grad_q, grad_k, error = pl.pallas_call(
        functools.partial(kernel, dims),
        out_shape=(
            jax.ShapeDtypeStruct((rows, heads * hd), BF16),
            jax.ShapeDtypeStruct((heads, feat, hd), F32),
            jax.ShapeDtypeStruct((heads, feat, hd), F32),
            jax.ShapeDtypeStruct((8, hd), F32),
        ),
        in_specs=[pl.BlockSpec(memory_space=pl.ANY)] * 5,
        out_specs=(vmem,) * 4,
        scratch_shapes=[
            pltpu.VMEM((rows, heads * hd), BF16),
            pltpu.VMEM((rows, hd), BF16),
            pltpu.VMEM((heads, feat, hd), BF16),
            pltpu.VMEM((heads, feat, hd), BF16),
            dma((5,)),
            pltpu.VMEM((heads, hd, rows), F32),
            pltpu.VMEM((heads, 1, rows), F32),
            pltpu.VMEM((16, hd), BF16),
            pltpu.VMEM((n, 16, hd), BF16),
            dma((n,)),
            dma((n,)),
            pltpu.VMEM((n, 2, rows, hd), BF16),
            pltpu.VMEM((heads * rows, hd), BF16),
            pltpu.VMEM((heads, 1, rows), F32),
            pltpu.VMEM((heads, 1, rows), F32),
            pltpu.VMEM((heads, hd, rows), F32),
            pltpu.VMEM((2 * hd, heads * feat2), F32),
            pltpu.VMEM((heads * feat2, 2 * hd), F32),
            pltpu.VMEM((heads, feat2, rows), F32),
            pltpu.VMEM((heads, feat2, rows), F32),
            pltpu.VMEM((heads, feat2, rows), F32),
            pltpu.VMEM((heads, feat2, rows), F32),
            pltpu.VMEM((state_pieces, piece, hd), BF16),
            pltpu.VMEM((n, piece, hd), BF16),
            pltpu.VMEM((n, piece, hd), BF16),
            pltpu.VMEM((state_pieces, piece, hd), BF16),
            pltpu.VMEM((grad_pieces, grad_rows, hd), BF16),
            pltpu.VMEM((n, grad_rows, hd), BF16),
            pltpu.VMEM((grad_pieces, grad_rows, hd), BF16),
            pltpu.VMEM((n, grad_rows, hd), BF16),
            pltpu.VMEM((2 * grad_rows, hd), BF16),
            pltpu.VMEM((grad_pieces, 2 * grad_rows, hd), BF16),
            pltpu.VMEM((8, hd), F32),
            pltpu.VMEM((heads_axis, 8, hd), F32),
            dma((levels,)),
            dma((levels,)),
            dma((2, levels)),
            dma((n,)),
            dma((n,)),
            dma((n,)),
            dma((n,)),
            dma((n,)),
            dma((n,)),
            dma((n,)),
            dma((n,)),
            dma((n,)),
            dma((n,)),
            dma((n,)),
            dma((heads_axis,)),
            dma((heads_axis,)),
        ],
        compiler_params=pltpu.CompilerParams(collective_id=0, has_side_effects=True),
    )(queries, keys, values, feat_q.swapaxes(1, 2), feat_k.swapaxes(1, 2))
    return student, grad_q.swapaxes(1, 2), grad_k.swapaxes(1, 2), error[0, 0]


def solution(mesh):
    in_specs = (
        P("ctx", "head"),
        P("ctx", "head"),
        P("ctx", "head"),
        P("head", None, None),
        P("head", None, None),
    )
    out_specs = (P("ctx", "head"), P("head", None, None), P("head", None, None), P())
    return jax.shard_map(
        on_device, mesh=mesh, in_specs=in_specs, out_specs=out_specs, check_vma=False
    )
```

```python
import functools
import math

import jax
import jax.numpy as jnp
from jax import lax
from jax.experimental import pallas as pl
from jax.experimental.pallas import tpu as pltpu
from jax.sharding import PartitionSpec as P

MESH = pl.DeviceIdType.MESH
F32 = jnp.float32
BF16 = jnp.bfloat16
PLANE = 4


def dot(a, b):
    return lax.dot_general(a, b, (((1,), (0,)), ((), ())), preferred_element_type=F32)


def dot_nt(a, b):
    return lax.dot_general(a, b, (((1,), (1,)), ((), ())), preferred_element_type=F32)


def feature_map(logits):
    high = jnp.max(logits, axis=0, keepdims=True)
    low = jnp.min(logits, axis=0, keepdims=True)
    pos = jnp.exp(logits - high)
    neg = jnp.exp(low - logits)
    pos = pos * (1.0 / jnp.sum(pos, axis=0, keepdims=True))
    neg = neg * (1.0 / jnp.sum(neg, axis=0, keepdims=True))
    return jnp.concatenate([pos, neg], axis=0)


def feature_grad(both, upstream):
    width = both.shape[0] // 2
    pos, neg = both[:width], both[width:]
    up_pos, up_neg = upstream[:width], upstream[width:]
    return pos * (up_pos - jnp.sum(up_pos * pos, axis=0, keepdims=True)) - neg * (
        up_neg - jnp.sum(up_neg * neg, axis=0, keepdims=True)
    )


def split(array):
    high = array.astype(BF16)
    return high, (array - high.astype(F32)).astype(BF16)


def kernel(
    dims,
    q_any, k_any, v_any, fq_any, fk_any,
    student_ref, gq_ref, gk_ref, err_ref,
    q_ref, v_ref, fq_ref, fk_ref, in_sem, numl, denl,
    kv, qs, top, total, acc, s_t, s_n, fqp, fkp, dfq, ldfk,
    st_out, st_in, st_fin, st_res, g_out, g_in, g_fin, g_res, e_out, e_in,
    z_send, x_send, c_send, kv_recv, a_send, a_recv, b_send, b_recv,
    k_send, k_recv, g_send, g_recv, e_send, e_recv,
):
    n, heads_axis, rows, heads, hd, feat, state_pieces, grad_pieces = dims
    me = lax.axis_index("ctx")
    my_head = lax.axis_index("head")
    feat2 = 2 * feat
    place = me % PLANE
    level = me // PLANE
    levels = n // PLANE
    core_mate = me + 1 - 2 * (me % 2)
    x_mate = me + 2 - 4 * ((me // 2) % 2)
    span = PLANE * rows

    def copy(src, dst, send, recv, target):
        return pltpu.make_async_remote_copy(
            src_ref=src, dst_ref=dst, send_sem=send, recv_sem=recv,
            device_id=(target, my_head), device_id_type=MESH,
        )

    def peers(body):
        if n <= 16:
            for k in range(1, n):
                body(lax.rem(me + k, n))
            return

        def step(k, carry):
            body(lax.rem(me + k, n))
            return carry

        lax.fori_loop(1, n, step, 0)

    def whole(ref, send, recv):
        part = ref.at[pl.ds(0, n - 1)]
        return copy(part, part, send, recv, core_mate)

    def head_mates(body):
        def step(k, carry):
            body((my_head + k) % heads_axis)
            return carry

        lax.fori_loop(1, heads_axis, step, 0)

    loads = [
        pltpu.make_async_copy(src, dst, in_sem.at[i])
        for i, (src, dst) in enumerate(
            ((k_any, kv.at[me, 0]), (v_any, v_ref), (fk_any, fk_ref), (q_any, q_ref), (fq_any, fq_ref))
        )
    ]
    for load in loads:
        load.start()

    barrier = pltpu.get_barrier_semaphore()
    peers(lambda p: pl.semaphore_signal(barrier, inc=1, device_id=(p, my_head), device_id_type=MESH))
    head_mates(lambda p: pl.semaphore_signal(barrier, inc=1, device_id=(me, p), device_id_type=MESH))
    loads[0].wait()
    loads[1].wait()
    v_t = v_ref[...].astype(F32).T.astype(BF16)
    kv[me, 1] = v_t
    pl.semaphore_wait(barrier, n - 1 + heads_axis - 1)

    def z_copy(up):
        return copy(kv.at[me], kv.at[me], z_send.at[up], kv_recv.at[me], up * PLANE + place)

    def kv_copy(block, send, target):
        return copy(kv.at[block], kv.at[block], send, kv_recv.at[block], target)

    def x_copy(h):
        return kv_copy(h * PLANE + place, x_send.at[h], x_mate)

    def c_copy(h):
        return kv_copy(h * PLANE + place, c_send.at[0, h], core_mate)

    def f_copy(h):
        return kv_copy(h * PLANE + x_mate % PLANE, c_send.at[1, h], core_mate)

    def kv_wait(block):
        kv_copy(block, z_send.at[0], core_mate).wait_recv()

    def loop(low, high, body):
        def step(i, carry):
            body(i)
            return carry

        lax.fori_loop(low, high, step, 0)

    x_copy(level).start()
    c_copy(level).start()
    loop(level + 1, levels, lambda up: z_copy(up).start())

    key_row = lax.broadcasted_iota(jnp.int32, (rows, rows), 0)
    query_col = lax.broadcasted_iota(jnp.int32, (rows, rows), 1)
    causal = key_row <= query_col
    for load in loads[2:]:
        load.wait()
    w_k = fk_ref[...].reshape(heads * feat, hd)
    w_q = fq_ref[...].reshape(heads * feat, hd)
    own_k = dot_nt(w_k, kv[me, 0])
    for g in range(heads):
        q_g = q_ref[:, g * hd : (g + 1) * hd]
        qs[g * rows : (g + 1) * rows, :] = q_g
        map_q = feature_map(dot_nt(w_q[g * feat : (g + 1) * feat], q_g))
        map_k = feature_map(own_k[g * feat : (g + 1) * feat])
        fqp[g] = map_q
        fkp[g] = map_k
        amat = jnp.where(causal, dot(map_k.T.astype(BF16), map_q.astype(BF16)), 0.0)
        numl[g] = dot(v_t, amat.astype(BF16))
        denl[g] = jnp.sum(amat, axis=0, keepdims=True)
    top[...] = jnp.full_like(top, -1e30)
    total[...] = jnp.zeros_like(total)
    acc[...] = jnp.zeros_like(acc)
    s_t[...] = jnp.zeros_like(s_t)
    s_n[...] = jnp.zeros_like(s_n)

    def relay(h):
        kv_wait(h * PLANE + place)
        x_copy(h).start()
        c_copy(h).start()

    def pass_on(h):
        kv_wait(h * PLANE + x_mate % PLANE)
        f_copy(h).start()

    scale = hd ** (-0.5) / math.log(2.0)
    ones = jnp.ones((hd, span), BF16)

    def absorb(t):
        h = level - t
        kv_wait(h * PLANE + core_mate % PLANE)
        kv_wait(h * PLANE + core_mate % PLANE + 2 - 4 * ((core_mate // 2) % 2))
        keys = kv[pl.ds(h * PLANE, PLANE), 0].reshape(span, hd)
        vals = jnp.concatenate([kv[h * PLANE + b, 1] for b in range(PLANE)], axis=1)
        key_pos = h * span + lax.broadcasted_iota(jnp.int32, (span, rows), 0)
        query_pos = me * rows + lax.broadcasted_iota(jnp.int32, (span, rows), 1)
        allowed = key_pos <= query_pos
        for g in range(heads):
            scores = dot_nt(keys, qs[g * rows : (g + 1) * rows, :])
            scores = jnp.where(allowed, scores, -1e30)
            old = top[g]
            new = jnp.maximum(old, jnp.max(scores, axis=0, keepdims=True))
            top[g] = new
            shrink = jnp.exp2((old - new) * scale)
            weights = jnp.exp2((scores - new) * scale)
            total[g] = total[g] * shrink + jnp.sum(weights, axis=0, keepdims=True)
            acc[g] = acc[g] * shrink + dot(vals, weights.astype(BF16))
        logits = dot_nt(fk_ref[...].reshape(heads * feat, hd), keys)
        before = h * span + lax.broadcasted_iota(jnp.int32, (feat2, span), 1) < me * rows
        maps = jnp.concatenate(
            [
                jnp.where(before, feature_map(logits[g * feat : (g + 1) * feat]), 0.0).astype(BF16)
                for g in range(heads)
            ],
            axis=0,
        )
        wide = jnp.concatenate([vals, ones], axis=0)
        s_t[...] += dot_nt(wide, maps)
        s_n[...] += dot_nt(maps, wide)

    def pipeline(u):
        pl.when(u <= level + 1)(lambda: pass_on(level - (u - 1)))
        pl.when(u <= level)(lambda: relay(level - u))
        pl.when(u >= 2)(lambda: absorb(u - 2))

    loop(1, level + 3, pipeline)

    per_head = state_pieces // heads
    piece = heads * feat2 // state_pieces
    squares = jnp.zeros((hd, rows), F32)
    norm_rows = []
    values = v_ref[...]
    for g in range(heads):
        fq_t = fqp[g].astype(BF16)
        fk_t = fkp[g].astype(BF16)
        high, low = split(s_t[:, g * feat2 : (g + 1) * feat2])
        prior = dot(jnp.concatenate([high, low], axis=1), jnp.concatenate([fq_t, fq_t], axis=0))
        numer = numl[g] + prior[:hd]
        denom = denl[g] + prior[hd : hd + 1]
        inverse = 1.0 / denom
        y = numer * inverse
        student_ref[:, g * hd : (g + 1) * hd] = y.T.astype(BF16)
        diff = y - acc[g] * (1.0 / total[g])
        squares = squares + diff * diff
        dy = 2.0 * diff
        dnumer = dy * inverse
        dden = -jnp.sum(dy * y, axis=0, keepdims=True) * inverse
        dnb = dnumer.astype(BF16)
        dmat = jnp.where(causal, dot(values, dnb) + dden, 0.0).astype(BF16)
        state = dot_nt(fq_t, dnb).astype(BF16)
        st_out[g * per_head : (g + 1) * per_head, :piece, :] = state.reshape(per_head, piece, hd)
        d_high, d_low = split(jnp.broadcast_to(dden, (16, rows)))
        norm_rows.append(dot_nt(d_high, fq_t) + dot_nt(d_low, fq_t))
        high, low = split(s_n[g * feat2 : (g + 1) * feat2, :hd])
        dfq[g] = (
            dot(jnp.concatenate([fk_t, high, low], axis=1), jnp.concatenate([dmat, dnb, dnb], axis=0))
            + s_n[g * feat2 : (g + 1) * feat2, hd:] * dden
        )
        ldfk[g] = dot_nt(fq_t, dmat)
    error = jnp.sum(jnp.sum(squares, axis=0, keepdims=True), axis=1, keepdims=True)
    first = error.astype(BF16).astype(F32)
    extra_row = lax.broadcasted_iota(jnp.int32, (16, hd), 0)
    extra = jnp.where(extra_row < 12, first, error - first)
    for g in range(heads):
        extra = jnp.where(extra_row == g, norm_rows[g], extra)
    extra = extra.astype(BF16)
    for p in range(n):
        st_out[p, piece:, :] = extra
        if p >= state_pieces:
            st_out[p, :piece, :] = jnp.zeros((piece, hd), BF16)

    def a_copy(p):
        return copy(st_out.at[p], st_in.at[me], a_send, a_recv, p)

    peers(lambda p: a_copy(p).start())
    st_in[me] = st_out[me]

    grad_rows = heads * feat // grad_pieces
    grad_per_head = grad_pieces // heads
    for g in range(heads):
        dlq = feature_grad(fqp[g], dfq[g]).astype(BF16)
        part = dot(dlq, qs[g * rows : (g + 1) * rows, :]).astype(BF16)
        g_out[g * grad_per_head : (g + 1) * grad_per_head, :grad_rows, :] = part.reshape(
            grad_per_head, grad_rows, hd
        )
    for p in range(grad_pieces, n):
        g_out[p] = jnp.zeros((2 * grad_rows, hd), BF16)

    def b_copy(d):
        return copy(st_fin.at[d], st_res.at[me], b_send, b_recv, d)

    whole(st_in, a_send, a_recv).wait_recv()

    def suffix(t, states):
        d = n - 1 - t
        st_fin[d] = states.astype(BF16)
        return states + st_in[d, :piece, :].astype(F32)

    lax.fori_loop(0, n, suffix, jnp.zeros((piece, hd), F32), unroll=n <= 16)
    peers(lambda d: b_copy(d).start())
    st_res[me] = st_fin[me]

    extras = st_in[:, piece:, :].astype(F32)
    later_norms = jnp.sum(
        jnp.where(lax.broadcasted_iota(jnp.int32, extras.shape, 0) > me, extras, 0.0), axis=0
    )
    summed = jnp.sum(jnp.where(extra_row < 8, 0.0, jnp.sum(extras, axis=0)), axis=0, keepdims=True)
    e_out[...] = jnp.broadcast_to(summed * 0.25, e_out.shape)

    def e_copy(p, s):
        return pltpu.make_async_remote_copy(
            src_ref=e_out, dst_ref=e_in.at[s], send_sem=e_send.at[p], recv_sem=e_recv.at[s],
            device_id=(me, p), device_id_type=MESH,
        )

    head_mates(lambda p: e_copy(p, my_head).start())
    for g in range(heads):
        norm = jnp.broadcast_to(later_norms[g : g + 1], (rows, feat2)).T
        ldfk[g] += norm

    whole(st_res, b_send, b_recv).wait_recv()
    for g in range(heads):
        later = st_res[g * per_head : (g + 1) * per_head].reshape(feat2, hd)
        dfk = ldfk[g] + dot(later, v_t)
        dlk = feature_grad(fkp[g], dfk).astype(BF16)
        part = dot(dlk, kv[me, 0]).astype(BF16)
        g_out[g * grad_per_head : (g + 1) * grad_per_head, grad_rows:, :] = part.reshape(
            grad_per_head, grad_rows, hd
        )

    def k_copy(p):
        return copy(g_out.at[p], g_in.at[me], k_send, k_recv, p)

    def g_copy(d):
        return copy(g_fin, g_res.at[me], g_send, g_recv, d)

    peers(lambda p: k_copy(p).start())
    g_in[me] = g_out[me]
    whole(g_in, k_send, k_recv).wait_recv()
    g_fin[...] = jnp.sum(g_in[...].astype(F32), axis=0).astype(BF16)
    peers(lambda d: g_copy(d).start())
    g_res[me] = g_fin[...]

    e_in[my_head] = e_out[...]
    head_mates(lambda s: e_copy(0, s).wait_recv())
    entries = n * rows * heads * heads_axis * hd
    err_ref[...] = jnp.sum(e_in[...], axis=0) / entries
    head_mates(lambda p: e_copy(p, my_head).wait_send())
    x_copy(level).wait_send()
    c_copy(level).wait_send()
    loop(level + 1, levels, lambda up: z_copy(up).wait_send())

    def relay_end(t):
        x_copy(t).wait_send()
        c_copy(t).wait_send()

    loop(0, level, relay_end)
    loop(0, level + 1, lambda t: f_copy(t).wait_send())
    whole(st_in, a_send, a_recv).wait_send()
    whole(st_res, b_send, b_recv).wait_send()
    whole(g_in, k_send, k_recv).wait_send()
    whole(g_res, g_send, g_recv).wait_recv()
    for g in range(heads):
        both = g_res[g * grad_per_head : (g + 1) * grad_per_head].astype(F32)
        gq_ref[g] = both[:, :grad_rows].reshape(feat, hd)
        gk_ref[g] = both[:, grad_rows:].reshape(feat, hd)
    whole(g_res, g_send, g_recv).wait_send()


def on_device(queries, keys, values, feat_q, feat_k):
    rows, hd = keys.shape
    heads, _, feat = feat_q.shape
    n = lax.axis_size("ctx")
    heads_axis = lax.axis_size("head")
    feat2 = 2 * feat
    state_pieces = min(n, heads * feat2 // 16)
    grad_pieces = min(n, heads * feat // 16)
    dims = (n, heads_axis, rows, heads, hd, feat, state_pieces, grad_pieces)
    piece = heads * feat2 // state_pieces
    grad_rows = heads * feat // grad_pieces
    levels = n // PLANE
    dma = pltpu.SemaphoreType.DMA
    vmem = pl.BlockSpec(memory_space=pltpu.VMEM)
    student, grad_q, grad_k, error = pl.pallas_call(
        functools.partial(kernel, dims),
        out_shape=(
            jax.ShapeDtypeStruct((rows, heads * hd), BF16),
            jax.ShapeDtypeStruct((heads, feat, hd), F32),
            jax.ShapeDtypeStruct((heads, feat, hd), F32),
            jax.ShapeDtypeStruct((8, hd), F32),
        ),
        in_specs=[pl.BlockSpec(memory_space=pltpu.HBM)] * 5,
        out_specs=(vmem,) * 4,
        scratch_shapes=[
            pltpu.VMEM((rows, heads * hd), BF16),
            pltpu.VMEM((rows, hd), BF16),
            pltpu.VMEM((heads, feat, hd), BF16),
            pltpu.VMEM((heads, feat, hd), BF16),
            dma((5,)),
            pltpu.VMEM((heads, hd, rows), F32),
            pltpu.VMEM((heads, 1, rows), F32),
            pltpu.VMEM((n, 2, rows, hd), BF16),
            pltpu.VMEM((heads * rows, hd), BF16),
            pltpu.VMEM((heads, 1, rows), F32),
            pltpu.VMEM((heads, 1, rows), F32),
            pltpu.VMEM((heads, hd, rows), F32),
            pltpu.VMEM((2 * hd, heads * feat2), F32),
            pltpu.VMEM((heads * feat2, 2 * hd), F32),
            pltpu.VMEM((heads, feat2, rows), F32),
            pltpu.VMEM((heads, feat2, rows), F32),
            pltpu.VMEM((heads, feat2, rows), F32),
            pltpu.VMEM((heads, feat2, rows), F32),
            pltpu.VMEM((n, piece + 16, hd), BF16),
            pltpu.VMEM((n, piece + 16, hd), BF16),
            pltpu.VMEM((n, piece, hd), BF16),
            pltpu.VMEM((n, piece, hd), BF16),
            pltpu.VMEM((n, 2 * grad_rows, hd), BF16),
            pltpu.VMEM((n, 2 * grad_rows, hd), BF16),
            pltpu.VMEM((2 * grad_rows, hd), BF16),
            pltpu.VMEM((n, 2 * grad_rows, hd), BF16),
            pltpu.VMEM((8, hd), F32),
            pltpu.VMEM((heads_axis, 8, hd), F32),
            dma((levels,)),
            dma((levels,)),
            dma((2, levels)),
            dma((n,)),
            dma(()),
            dma(()),
            dma(()),
            dma(()),
            dma(()),
            dma(()),
            dma(()),
            dma(()),
            dma((heads_axis,)),
            dma((heads_axis,)),
        ],
        compiler_params=pltpu.CompilerParams(
            collective_id=0, has_side_effects=True, vmem_limit_bytes=40 * 1024 * 1024
        ),
    )(queries, keys, values, feat_q.swapaxes(1, 2), feat_k.swapaxes(1, 2))
    return student, grad_q.swapaxes(1, 2), grad_k.swapaxes(1, 2), error[0, 0]


def solution(mesh):
    in_specs = (
        P("ctx", "head"),
        P("ctx", "head"),
        P("ctx", "head"),
        P("head", None, None),
        P("head", None, None),
    )
    out_specs = (P("ctx", "head"), P("head", None, None), P("head", None, None), P())
    return jax.shard_map(
        on_device, mesh=mesh, in_specs=in_specs, out_specs=out_specs, check_vma=False
    )
```

```python
import functools
import math

import jax
import jax.numpy as jnp
from jax import lax
from jax.experimental import pallas as pl
from jax.experimental.pallas import tpu as pltpu
from jax.sharding import PartitionSpec as P

MESH = pl.DeviceIdType.MESH
F32 = jnp.float32
BF16 = jnp.bfloat16
PLANE = 4


def dot(a, b):
    return lax.dot_general(a, b, (((1,), (0,)), ((), ())), preferred_element_type=F32)


def dot_nt(a, b):
    return lax.dot_general(a, b, (((1,), (1,)), ((), ())), preferred_element_type=F32)


def feature_map(logits):
    high = jnp.max(logits, axis=0, keepdims=True)
    low = jnp.min(logits, axis=0, keepdims=True)
    pos = jnp.exp(logits - high)
    neg = jnp.exp(low - logits)
    pos = pos * (1.0 / jnp.sum(pos, axis=0, keepdims=True))
    neg = neg * (1.0 / jnp.sum(neg, axis=0, keepdims=True))
    return jnp.concatenate([pos, neg], axis=0)


def feature_grad(both, upstream):
    width = both.shape[0] // 2
    pos, neg = both[:width], both[width:]
    up_pos, up_neg = upstream[:width], upstream[width:]
    return pos * (up_pos - jnp.sum(up_pos * pos, axis=0, keepdims=True)) - neg * (
        up_neg - jnp.sum(up_neg * neg, axis=0, keepdims=True)
    )


def split(array):
    high = array.astype(BF16)
    return high, (array - high.astype(F32)).astype(BF16)


def kernel(
    dims,
    q_ref, k_ref, v_ref, fq_ref, fk_ref,
    student_ref, gq_ref, gk_ref, err_ref,
    numl, denl, x_out, x_in, n_send, n_recv, q_send, q_recv,
    kv, qs, top, total, acc, s_t, s_n, fqp, fkp, dfq, ldfk,
    st_out, st_in, st_fin, st_res, gq_out, gq_in, gk_out, gk_in, g_fin, g_res, e_out, e_in,
    z_send, x_send, c_send, kv_recv, a_send, a_recv, b_send, b_recv,
    k_send, k_recv, g_send, g_recv, e_send, e_recv,
):
    n, heads_axis, rows, heads, hd, feat, state_pieces, grad_pieces = dims
    me = lax.axis_index("ctx")
    my_head = lax.axis_index("head")
    feat2 = 2 * feat
    place = me % PLANE
    level = me // PLANE
    levels = n // PLANE
    core_mate = me + 1 - 2 * (me % 2)
    x_mate = me + 2 - 4 * ((me // 2) % 2)
    span = PLANE * rows

    def copy(src, dst, send, recv, target):
        return pltpu.make_async_remote_copy(
            src_ref=src, dst_ref=dst, send_sem=send, recv_sem=recv,
            device_id=(target, my_head), device_id_type=MESH,
        )

    def peers(body):
        if n <= 16:
            for k in range(1, n):
                body(lax.rem(me + k, n))
            return

        def step(k, carry):
            body(lax.rem(me + k, n))
            return carry

        lax.fori_loop(1, n, step, 0)

    def whole(ref, send, recv):
        part = ref.at[pl.ds(0, n - 1)]
        return copy(part, part, send, recv, core_mate)

    def head_mates(body):
        def step(k, carry):
            body((my_head + k) % heads_axis)
            return carry

        lax.fori_loop(1, heads_axis, step, 0)

    barrier = pltpu.get_barrier_semaphore()
    peers(lambda p: pl.semaphore_signal(barrier, inc=1, device_id=(p, my_head), device_id_type=MESH))
    head_mates(lambda p: pl.semaphore_signal(barrier, inc=1, device_id=(me, p), device_id_type=MESH))
    kv[me, 0] = k_ref[...]
    v_t = v_ref[...].astype(F32).T.astype(BF16)
    kv[me, 1] = v_t
    pl.semaphore_wait(barrier, n - 1 + heads_axis - 1)

    def z_copy(up):
        return copy(kv.at[me], kv.at[me], z_send.at[up], kv_recv.at[me], up * PLANE + place)

    def kv_copy(block, send, target):
        return copy(kv.at[block], kv.at[block], send, kv_recv.at[block], target)

    def x_copy(h):
        return kv_copy(h * PLANE + place, x_send.at[h], x_mate)

    def c_copy(h):
        return kv_copy(h * PLANE + place, c_send.at[0, h], core_mate)

    def f_copy(h):
        return kv_copy(h * PLANE + x_mate % PLANE, c_send.at[1, h], core_mate)

    def kv_wait(block):
        kv_copy(block, z_send.at[0], core_mate).wait_recv()

    def loop(low, high, body):
        def step(i, carry):
            body(i)
            return carry

        lax.fori_loop(low, high, step, 0)

    x_copy(level).start()
    c_copy(level).start()
    loop(level + 1, levels, lambda up: z_copy(up).start())

    key_row = lax.broadcasted_iota(jnp.int32, (rows, rows), 0)
    query_col = lax.broadcasted_iota(jnp.int32, (rows, rows), 1)
    causal = key_row <= query_col
    w_k = fk_ref[...].reshape(heads * feat, hd)
    w_q = fq_ref[...].reshape(heads * feat, hd)
    own_k = dot_nt(w_k, k_ref[...])
    for g in range(heads):
        q_g = q_ref[:, g * hd : (g + 1) * hd]
        qs[g * rows : (g + 1) * rows, :] = q_g
        map_q = feature_map(dot_nt(w_q[g * feat : (g + 1) * feat], q_g))
        map_k = feature_map(own_k[g * feat : (g + 1) * feat])
        fqp[g] = map_q
        fkp[g] = map_k
        amat = jnp.where(causal, dot(map_k.T.astype(BF16), map_q.astype(BF16)), 0.0)
        numl[g] = dot(v_t, amat.astype(BF16))
        denl[g] = jnp.sum(amat, axis=0, keepdims=True)
    top[...] = jnp.full_like(top, -1e30)
    total[...] = jnp.zeros_like(total)
    acc[...] = jnp.zeros_like(acc)
    s_t[...] = jnp.zeros_like(s_t)
    s_n[...] = jnp.zeros_like(s_n)

    def relay(h):
        kv_wait(h * PLANE + place)
        x_copy(h).start()
        c_copy(h).start()

    def pass_on(h):
        kv_wait(h * PLANE + x_mate % PLANE)
        f_copy(h).start()

    scale = hd ** (-0.5) / math.log(2.0)
    ones = jnp.ones((hd, span), BF16)

    def absorb(t):
        h = level - t
        kv_wait(h * PLANE + core_mate % PLANE)
        kv_wait(h * PLANE + core_mate % PLANE + 2 - 4 * ((core_mate // 2) % 2))
        keys = kv[pl.ds(h * PLANE, PLANE), 0].reshape(span, hd)
        vals = jnp.concatenate([kv[h * PLANE + b, 1] for b in range(PLANE)], axis=1)
        key_pos = h * span + lax.broadcasted_iota(jnp.int32, (span, rows), 0)
        query_pos = me * rows + lax.broadcasted_iota(jnp.int32, (span, rows), 1)
        allowed = key_pos <= query_pos
        for g in range(heads):
            scores = dot_nt(keys, qs[g * rows : (g + 1) * rows, :])
            scores = jnp.where(allowed, scores, -1e30)
            old = top[g]
            new = jnp.maximum(old, jnp.max(scores, axis=0, keepdims=True))
            top[g] = new
            shrink = jnp.exp2((old - new) * scale)
            weights = jnp.exp2((scores - new) * scale)
            total[g] = total[g] * shrink + jnp.sum(weights, axis=0, keepdims=True)
            acc[g] = acc[g] * shrink + dot(vals, weights.astype(BF16))
        logits = dot_nt(fk_ref[...].reshape(heads * feat, hd), keys)
        before = h * span + lax.broadcasted_iota(jnp.int32, (feat2, span), 1) < me * rows
        maps = jnp.concatenate(
            [
                jnp.where(before, feature_map(logits[g * feat : (g + 1) * feat]), 0.0).astype(BF16)
                for g in range(heads)
            ],
            axis=0,
        )
        wide = jnp.concatenate([vals, ones], axis=0)
        s_t[...] += dot_nt(wide, maps)
        s_n[...] += dot_nt(maps, wide)

    def pipeline(u):
        pl.when(u <= level + 1)(lambda: pass_on(level - (u - 1)))
        pl.when(u <= level)(lambda: relay(level - u))
        pl.when(u >= 2)(lambda: absorb(u - 2))

    loop(1, level + 3, pipeline)

    per_head = state_pieces // heads
    piece = heads * feat2 // state_pieces
    squares = jnp.zeros((hd, rows), F32)
    norm_rows = {}
    order = [*range(0, heads, 2), *range(1, heads, 2)]

    def a_copy(p):
        return copy(st_out.at[p], st_in.at[me], a_send, a_recv, p)

    def to_others(targets, start):
        for p in targets:
            pl.when(me != p)(lambda p=p: start(p).start())

    values = v_ref[...]
    for p in range(state_pieces, n):
        st_out[p] = jnp.zeros((piece, hd), BF16)
    to_others(range(state_pieces, n), a_copy)
    for g in order:
        fq_t = fqp[g].astype(BF16)
        fk_t = fkp[g].astype(BF16)
        high, low = split(s_t[:, g * feat2 : (g + 1) * feat2])
        prior = dot(jnp.concatenate([high, low], axis=1), jnp.concatenate([fq_t, fq_t], axis=0))
        numer = numl[g] + prior[:hd]
        denom = denl[g] + prior[hd : hd + 1]
        inverse = 1.0 / denom
        y = numer * inverse
        student_ref[:, g * hd : (g + 1) * hd] = y.T.astype(BF16)
        diff = y - acc[g] * (1.0 / total[g])
        squares = squares + diff * diff
        dy = 2.0 * diff
        dnumer = dy * inverse
        dden = -jnp.sum(dy * y, axis=0, keepdims=True) * inverse
        dnb = dnumer.astype(BF16)
        dmat = jnp.where(causal, dot(values, dnb) + dden, 0.0).astype(BF16)
        state = dot_nt(fq_t, dnb).astype(BF16)
        for j in range(per_head):
            st_out[j * heads + g] = state[j * piece : (j + 1) * piece]
        to_others(range(g, state_pieces, heads), a_copy)
        d_high, d_low = split(jnp.broadcast_to(dden, (16, rows)))
        norm_rows[g] = dot_nt(d_high, fq_t) + dot_nt(d_low, fq_t)
        high, low = split(s_n[g * feat2 : (g + 1) * feat2, :hd])
        dfq[g] = (
            dot(jnp.concatenate([fk_t, high, low], axis=1), jnp.concatenate([dmat, dnb, dnb], axis=0))
            + s_n[g * feat2 : (g + 1) * feat2, hd:] * dden
        )
        ldfk[g] = dot_nt(fq_t, dmat)
    error = jnp.sum(jnp.sum(squares, axis=0, keepdims=True), axis=1, keepdims=True)
    first = error.astype(BF16).astype(F32)
    extra_row = lax.broadcasted_iota(jnp.int32, (16, hd), 0)
    extra = jnp.where(extra_row < 12, first, error - first)
    for g in range(heads):
        extra = jnp.where(extra_row == g, norm_rows[g], extra)
    x_out[...] = extra.astype(BF16)

    def n_copy(p):
        return copy(x_out, x_in.at[me], n_send, n_recv, p)

    peers(lambda p: n_copy(p).start())
    st_in[me] = st_out[me]
    x_in[me] = x_out[...]

    grad_rows = heads * feat // grad_pieces
    grad_per_head = grad_pieces // heads
    for g in range(heads):
        dlq = feature_grad(fqp[g], dfq[g]).astype(BF16)
        part = dot(dlq, qs[g * rows : (g + 1) * rows, :]).astype(BF16)
        for j in range(grad_per_head):
            gq_out[j * heads + g] = part[j * grad_rows : (j + 1) * grad_rows]
    for p in range(grad_pieces, n):
        gq_out[p] = jnp.zeros((grad_rows, hd), BF16)
        gk_out[p] = jnp.zeros((grad_rows, hd), BF16)

    def q_copy(p):
        return copy(gq_out.at[p], gq_in.at[me], q_send, q_recv, p)

    def k_copy(p):
        return copy(gk_out.at[p], gk_in.at[me], k_send, k_recv, p)

    def b_copy(d):
        return copy(st_fin.at[d], st_res.at[me], b_send, b_recv, d)

    whole(st_in, a_send, a_recv).wait_recv()

    def suffix(t, states):
        d = n - 1 - t
        st_fin[d] = states.astype(BF16)
        return states + st_in[d].astype(F32)

    lax.fori_loop(0, n, suffix, jnp.zeros((piece, hd), F32), unroll=n <= 16)
    peers(lambda d: b_copy(d).start())
    peers(lambda p: q_copy(p).start())
    to_others(range(grad_pieces, n), k_copy)
    gq_in[me] = gq_out[me]
    st_res[me] = st_fin[me]

    whole(x_in, n_send, n_recv).wait_recv()
    extras = x_in[...].astype(F32)
    later_norms = jnp.sum(
        jnp.where(lax.broadcasted_iota(jnp.int32, extras.shape, 0) > me, extras, 0.0), axis=0
    )
    summed = jnp.sum(jnp.where(extra_row < 8, 0.0, jnp.sum(extras, axis=0)), axis=0, keepdims=True)
    e_out[...] = jnp.broadcast_to(summed * 0.25, e_out.shape)

    def e_copy(p, s):
        return pltpu.make_async_remote_copy(
            src_ref=e_out, dst_ref=e_in.at[s], send_sem=e_send.at[p], recv_sem=e_recv.at[s],
            device_id=(me, p), device_id_type=MESH,
        )

    head_mates(lambda p: e_copy(p, my_head).start())
    for g in range(heads):
        norm = jnp.broadcast_to(later_norms[g : g + 1], (rows, feat2)).T
        ldfk[g] += norm

    whole(st_res, b_send, b_recv).wait_recv()
    for g in order:
        later = jnp.concatenate([st_res[j * heads + g] for j in range(per_head)], axis=0)
        dfk = ldfk[g] + dot(later, v_t)
        dlk = feature_grad(fkp[g], dfk).astype(BF16)
        part = dot(dlk, k_ref[...]).astype(BF16)
        for j in range(grad_per_head):
            gk_out[j * heads + g] = part[j * grad_rows : (j + 1) * grad_rows]
        to_others(range(g, grad_pieces, heads), k_copy)

    def g_copy(d):
        return copy(g_fin, g_res.at[me], g_send, g_recv, d)

    gk_in[me] = gk_out[me]
    whole(gq_in, q_send, q_recv).wait_recv()
    g_fin[:grad_rows] = jnp.sum(gq_in[...].astype(F32), axis=0).astype(BF16)
    whole(gk_in, k_send, k_recv).wait_recv()
    g_fin[grad_rows:] = jnp.sum(gk_in[...].astype(F32), axis=0).astype(BF16)
    peers(lambda d: g_copy(d).start())
    g_res[me] = g_fin[...]

    e_in[my_head] = e_out[...]
    head_mates(lambda s: e_copy(0, s).wait_recv())
    entries = n * rows * heads * heads_axis * hd
    err_ref[...] = jnp.sum(e_in[...], axis=0) / entries
    head_mates(lambda p: e_copy(p, my_head).wait_send())
    x_copy(level).wait_send()
    c_copy(level).wait_send()
    loop(level + 1, levels, lambda up: z_copy(up).wait_send())

    def relay_end(t):
        x_copy(t).wait_send()
        c_copy(t).wait_send()

    loop(0, level, relay_end)
    loop(0, level + 1, lambda t: f_copy(t).wait_send())
    whole(st_in, a_send, a_recv).wait_send()
    whole(st_res, b_send, b_recv).wait_send()
    whole(x_in, n_send, n_recv).wait_send()
    whole(gq_in, q_send, q_recv).wait_send()
    whole(gk_in, k_send, k_recv).wait_send()
    whole(g_res, g_send, g_recv).wait_recv()
    for g in range(heads):
        both = jnp.stack([g_res[j * heads + g] for j in range(grad_per_head)]).astype(F32)
        gq_ref[g] = both[:, :grad_rows].reshape(feat, hd)
        gk_ref[g] = both[:, grad_rows:].reshape(feat, hd)
    whole(g_res, g_send, g_recv).wait_send()


def on_device(queries, keys, values, feat_q, feat_k):
    rows, hd = keys.shape
    heads, _, feat = feat_q.shape
    n = lax.axis_size("ctx")
    heads_axis = lax.axis_size("head")
    feat2 = 2 * feat
    state_pieces = min(n, heads * feat2 // 16)
    grad_pieces = min(n, heads * feat // 16)
    dims = (n, heads_axis, rows, heads, hd, feat, state_pieces, grad_pieces)
    piece = heads * feat2 // state_pieces
    grad_rows = heads * feat // grad_pieces
    levels = n // PLANE
    dma = pltpu.SemaphoreType.DMA
    vmem = pl.BlockSpec(memory_space=pltpu.VMEM)
    student, grad_q, grad_k, error = pl.pallas_call(
        functools.partial(kernel, dims),
        out_shape=(
            jax.ShapeDtypeStruct((rows, heads * hd), BF16),
            jax.ShapeDtypeStruct((heads, feat, hd), F32),
            jax.ShapeDtypeStruct((heads, feat, hd), F32),
            jax.ShapeDtypeStruct((8, hd), F32),
        ),
        in_specs=[vmem] * 5,
        out_specs=(vmem,) * 4,
        scratch_shapes=[
            pltpu.VMEM((heads, hd, rows), F32),
            pltpu.VMEM((heads, 1, rows), F32),
            pltpu.VMEM((16, hd), BF16),
            pltpu.VMEM((n, 16, hd), BF16),
            dma(()),
            dma(()),
            dma(()),
            dma(()),
            pltpu.VMEM((n, 2, rows, hd), BF16),
            pltpu.VMEM((heads * rows, hd), BF16),
            pltpu.VMEM((heads, 1, rows), F32),
            pltpu.VMEM((heads, 1, rows), F32),
            pltpu.VMEM((heads, hd, rows), F32),
            pltpu.VMEM((2 * hd, heads * feat2), F32),
            pltpu.VMEM((heads * feat2, 2 * hd), F32),
            pltpu.VMEM((heads, feat2, rows), F32),
            pltpu.VMEM((heads, feat2, rows), F32),
            pltpu.VMEM((heads, feat2, rows), F32),
            pltpu.VMEM((heads, feat2, rows), F32),
            pltpu.VMEM((n, piece, hd), BF16),
            pltpu.VMEM((n, piece, hd), BF16),
            pltpu.VMEM((n, piece, hd), BF16),
            pltpu.VMEM((n, piece, hd), BF16),
            pltpu.VMEM((n, grad_rows, hd), BF16),
            pltpu.VMEM((n, grad_rows, hd), BF16),
            pltpu.VMEM((n, grad_rows, hd), BF16),
            pltpu.VMEM((n, grad_rows, hd), BF16),
            pltpu.VMEM((2 * grad_rows, hd), BF16),
            pltpu.VMEM((n, 2 * grad_rows, hd), BF16),
            pltpu.VMEM((8, hd), F32),
            pltpu.VMEM((heads_axis, 8, hd), F32),
            dma((levels,)),
            dma((levels,)),
            dma((2, levels)),
            dma((n,)),
            dma(()),
            dma(()),
            dma(()),
            dma(()),
            dma(()),
            dma(()),
            dma(()),
            dma(()),
            dma((heads_axis,)),
            dma((heads_axis,)),
        ],
        compiler_params=pltpu.CompilerParams(
            collective_id=0, has_side_effects=True, vmem_limit_bytes=40 * 1024 * 1024
        ),
    )(queries, keys, values, feat_q.swapaxes(1, 2), feat_k.swapaxes(1, 2))
    return student, grad_q.swapaxes(1, 2), grad_k.swapaxes(1, 2), error[0, 0]


def solution(mesh):
    in_specs = (
        P("ctx", "head"),
        P("ctx", "head"),
        P("ctx", "head"),
        P("head", None, None),
        P("head", None, None),
    )
    out_specs = (P("ctx", "head"), P("head", None, None), P("head", None, None), P())
    return jax.shard_map(
        on_device, mesh=mesh, in_specs=in_specs, out_specs=out_specs, check_vma=False
    )
```

```python
import functools
import math

import jax
import jax.numpy as jnp
from jax import lax
from jax.experimental import pallas as pl
from jax.experimental.pallas import tpu as pltpu
from jax.sharding import PartitionSpec as P

MESH = pl.DeviceIdType.MESH
F32 = jnp.float32
BF16 = jnp.bfloat16
PLANE = 4


def dot(a, b):
    return lax.dot_general(a, b, (((1,), (0,)), ((), ())), preferred_element_type=F32)


def dot_nt(a, b):
    return lax.dot_general(a, b, (((1,), (1,)), ((), ())), preferred_element_type=F32)


def feature_map(logits):
    high = jnp.max(logits, axis=0, keepdims=True)
    low = jnp.min(logits, axis=0, keepdims=True)
    pos = jnp.exp(logits - high)
    neg = jnp.exp(low - logits)
    pos = pos * (1.0 / jnp.sum(pos, axis=0, keepdims=True))
    neg = neg * (1.0 / jnp.sum(neg, axis=0, keepdims=True))
    return jnp.concatenate([pos, neg], axis=0)


def feature_grad(both, upstream):
    width = both.shape[0] // 2
    pos, neg = both[:width], both[width:]
    up_pos, up_neg = upstream[:width], upstream[width:]
    return pos * (up_pos - jnp.sum(up_pos * pos, axis=0, keepdims=True)) - neg * (
        up_neg - jnp.sum(up_neg * neg, axis=0, keepdims=True)
    )


def split(array):
    high = array.astype(BF16)
    return high, (array - high.astype(F32)).astype(BF16)


def kernel(
    dims,
    q_ref, k_ref, v_ref, fq_ref, fk_ref,
    student_ref, gq_ref, gk_ref, err_ref,
    numl, denl, x_out, x_in, n_send, n_recv, q_send, q_recv,
    kv, qs, top, total, acc, s_t, s_n, fqp, fkp, dfq, ldfk,
    st_out, st_in, st_fin, st_res, gq_out, gq_in, gk_out, gk_in, g_fin, g_res, e_out, e_in,
    z_send, x_send, c_send, kv_recv, a_send, a_recv, b_send, b_recv,
    k_send, k_recv, g_send, g_recv, e_send, e_recv,
):
    n, heads_axis, rows, heads, hd, feat, state_pieces, grad_pieces = dims
    me = lax.axis_index("ctx")
    my_head = lax.axis_index("head")
    feat2 = 2 * feat
    place = me % PLANE
    level = me // PLANE
    levels = n // PLANE
    core_mate = me + 1 - 2 * (me % 2)
    x_mate = me + 2 - 4 * ((me // 2) % 2)
    span = PLANE * rows

    def copy(src, dst, send, recv, target):
        return pltpu.make_async_remote_copy(
            src_ref=src, dst_ref=dst, send_sem=send, recv_sem=recv,
            device_id=(target, my_head), device_id_type=MESH,
        )

    def peers(body):
        if n <= 16:
            for k in range(1, n):
                body(lax.rem(me + k, n))
            return

        def step(k, carry):
            body(lax.rem(me + k, n))
            return carry

        lax.fori_loop(1, n, step, 0)

    def whole(ref, send, recv):
        part = ref.at[pl.ds(0, n - 1)]
        return copy(part, part, send, recv, core_mate)

    def head_mates(body):
        def step(k, carry):
            body((my_head + k) % heads_axis)
            return carry

        lax.fori_loop(1, heads_axis, step, 0)

    barrier = pltpu.get_barrier_semaphore()
    peers(lambda p: pl.semaphore_signal(barrier, inc=1, device_id=(p, my_head), device_id_type=MESH))
    head_mates(lambda p: pl.semaphore_signal(barrier, inc=1, device_id=(me, p), device_id_type=MESH))
    kv[me, 0] = k_ref[...]
    v_t = v_ref[...].astype(F32).T.astype(BF16)
    kv[me, 1] = v_t
    pl.semaphore_wait(barrier, n - 1 + heads_axis - 1)

    def z_copy(up):
        return copy(kv.at[me], kv.at[me], z_send.at[up], kv_recv.at[me], up * PLANE + place)

    def kv_copy(block, send, target):
        return copy(kv.at[block], kv.at[block], send, kv_recv.at[block], target)

    def x_copy(h):
        return kv_copy(h * PLANE + place, x_send.at[h], x_mate)

    def c_copy(h):
        return kv_copy(h * PLANE + place, c_send.at[0, h], core_mate)

    def f_copy(h):
        return kv_copy(h * PLANE + x_mate % PLANE, c_send.at[1, h], core_mate)

    def kv_wait(block):
        kv_copy(block, z_send.at[0], core_mate).wait_recv()

    def loop(low, high, body):
        def step(i, carry):
            body(i)
            return carry

        lax.fori_loop(low, high, step, 0)

    x_copy(level).start()
    c_copy(level).start()
    loop(level + 1, levels, lambda up: z_copy(up).start())

    key_row = lax.broadcasted_iota(jnp.int32, (rows, rows), 0)
    query_col = lax.broadcasted_iota(jnp.int32, (rows, rows), 1)
    causal = key_row <= query_col
    w_k = fk_ref[...].reshape(heads * feat, hd)
    w_q = fq_ref[...].reshape(heads * feat, hd)
    own_k = dot_nt(w_k, k_ref[...])
    for g in range(heads):
        q_g = q_ref[:, g * hd : (g + 1) * hd]
        qs[g * rows : (g + 1) * rows, :] = q_g
        map_q = feature_map(dot_nt(w_q[g * feat : (g + 1) * feat], q_g))
        map_k = feature_map(own_k[g * feat : (g + 1) * feat])
        fqp[g] = map_q
        fkp[g] = map_k
        amat = jnp.where(causal, dot(map_k.T.astype(BF16), map_q.astype(BF16)), 0.0)
        numl[g] = dot(v_t, amat.astype(BF16))
        denl[g] = jnp.sum(amat, axis=0, keepdims=True)
    top[...] = jnp.full_like(top, -1e30)
    total[...] = jnp.zeros_like(total)
    acc[...] = jnp.zeros_like(acc)
    s_t[...] = jnp.zeros_like(s_t)
    s_n[...] = jnp.zeros_like(s_n)

    def relay(h):
        kv_wait(h * PLANE + place)
        x_copy(h).start()
        c_copy(h).start()

    def pass_on(h):
        kv_wait(h * PLANE + x_mate % PLANE)
        f_copy(h).start()

    scale = hd ** (-0.5) / math.log(2.0)
    ones = jnp.ones((hd, span), BF16)

    def absorb(t):
        h = level - t
        kv_wait(h * PLANE + core_mate % PLANE)
        kv_wait(h * PLANE + core_mate % PLANE + 2 - 4 * ((core_mate // 2) % 2))
        keys = kv[pl.ds(h * PLANE, PLANE), 0].reshape(span, hd)
        vals = jnp.concatenate([kv[h * PLANE + b, 1] for b in range(PLANE)], axis=1)
        key_pos = h * span + lax.broadcasted_iota(jnp.int32, (span, rows), 0)
        query_pos = me * rows + lax.broadcasted_iota(jnp.int32, (span, rows), 1)
        allowed = key_pos <= query_pos
        for g in range(heads):
            scores = dot_nt(keys, qs[g * rows : (g + 1) * rows, :])
            scores = jnp.where(allowed, scores, -1e30)
            old = top[g]
            new = jnp.maximum(old, jnp.max(scores, axis=0, keepdims=True))
            top[g] = new
            shrink = jnp.exp2((old - new) * scale)
            weights = jnp.exp2((scores - new) * scale)
            total[g] = total[g] * shrink + jnp.sum(weights, axis=0, keepdims=True)
            acc[g] = acc[g] * shrink + dot(vals, weights.astype(BF16))
        logits = dot_nt(fk_ref[...].reshape(heads * feat, hd), keys)
        before = h * span + lax.broadcasted_iota(jnp.int32, (feat2, span), 1) < me * rows
        maps = jnp.concatenate(
            [
                jnp.where(before, feature_map(logits[g * feat : (g + 1) * feat]), 0.0).astype(BF16)
                for g in range(heads)
            ],
            axis=0,
        )
        wide = jnp.concatenate([vals, ones], axis=0)
        s_t[...] += dot_nt(wide, maps)
        s_n[...] += dot_nt(maps, wide)

    def pipeline(u):
        pl.when(u <= level + 1)(lambda: pass_on(level - (u - 1)))
        pl.when(u <= level)(lambda: relay(level - u))
        pl.when(u >= 2)(lambda: absorb(u - 2))

    loop(1, level + 3, pipeline)

    per_head = state_pieces // heads
    piece = heads * feat2 // state_pieces
    squares = jnp.zeros((hd, rows), F32)
    norm_rows = {}
    order = [*range(0, heads, 2), *range(1, heads, 2)]

    def a_copy(p):
        return copy(st_out.at[p], st_in.at[me], a_send, a_recv, p)

    def to_others(targets, start):
        for p in targets:
            pl.when(me != p)(lambda p=p: start(p).start())

    values = v_ref[...]
    for p in range(state_pieces, n):
        st_out[p] = jnp.zeros((piece, hd), BF16)
    to_others(range(state_pieces, n), a_copy)
    for g in order:
        fq_t = fqp[g].astype(BF16)
        fk_t = fkp[g].astype(BF16)
        high, low = split(s_t[:, g * feat2 : (g + 1) * feat2])
        prior = dot(jnp.concatenate([high, low], axis=1), jnp.concatenate([fq_t, fq_t], axis=0))
        numer = numl[g] + prior[:hd]
        denom = denl[g] + prior[hd : hd + 1]
        inverse = 1.0 / denom
        y = numer * inverse
        student_ref[:, g * hd : (g + 1) * hd] = y.T.astype(BF16)
        diff = y - acc[g] * (1.0 / total[g])
        squares = squares + diff * diff
        dy = 2.0 * diff
        dnumer = dy * inverse
        dden = -jnp.sum(dy * y, axis=0, keepdims=True) * inverse
        dnb = dnumer.astype(BF16)
        dmat = jnp.where(causal, dot(values, dnb) + dden, 0.0).astype(BF16)
        state = dot_nt(fq_t, dnb).astype(BF16)
        for j in range(per_head):
            st_out[j * heads + g] = state[j * piece : (j + 1) * piece]
        to_others(range(g, state_pieces, heads), a_copy)
        d_high, d_low = split(jnp.broadcast_to(dden, (16, rows)))
        norm_rows[g] = dot_nt(d_high, fq_t) + dot_nt(d_low, fq_t)
        high, low = split(s_n[g * feat2 : (g + 1) * feat2, :hd])
        dfq[g] = (
            dot(jnp.concatenate([fk_t, high, low], axis=1), jnp.concatenate([dmat, dnb, dnb], axis=0))
            + s_n[g * feat2 : (g + 1) * feat2, hd:] * dden
        )
        ldfk[g] = dot_nt(fq_t, dmat)
    error = jnp.sum(jnp.sum(squares, axis=0, keepdims=True), axis=1, keepdims=True)
    first = error.astype(BF16).astype(F32)
    extra_row = lax.broadcasted_iota(jnp.int32, (16, hd), 0)
    extra = jnp.where(extra_row < 12, first, error - first)
    for g in range(heads):
        extra = jnp.where(extra_row == g, norm_rows[g], extra)
    x_out[...] = extra.astype(BF16)

    def n_copy(p):
        return copy(x_out, x_in.at[me], n_send, n_recv, p)

    peers(lambda p: n_copy(p).start())
    st_in[me] = st_out[me]
    x_in[me] = x_out[...]

    grad_rows = heads * feat // grad_pieces
    grad_per_head = grad_pieces // heads
    for g in range(heads):
        dlq = feature_grad(fqp[g], dfq[g]).astype(BF16)
        part = dot(dlq, qs[g * rows : (g + 1) * rows, :]).astype(BF16)
        for j in range(grad_per_head):
            gq_out[j * heads + g] = part[j * grad_rows : (j + 1) * grad_rows]
    for p in range(grad_pieces, n):
        gq_out[p] = jnp.zeros((grad_rows, hd), BF16)
        gk_out[p] = jnp.zeros((grad_rows, hd), BF16)

    def q_copy(p):
        return copy(gq_out.at[p], gq_in.at[me], q_send, q_recv, p)

    def k_copy(p):
        return copy(gk_out.at[p], gk_in.at[me], k_send, k_recv, p)

    def b_copy(d):
        return copy(st_fin.at[d], st_res.at[me], b_send, b_recv, d)

    whole(st_in, a_send, a_recv).wait_recv()

    def suffix(t, states):
        d = n - 1 - t
        st_fin[d] = states.astype(BF16)
        return states + st_in[d].astype(F32)

    lax.fori_loop(0, n, suffix, jnp.zeros((piece, hd), F32), unroll=n <= 16)
    peers(lambda d: b_copy(d).start())
    peers(lambda p: q_copy(p).start())
    to_others(range(grad_pieces, n), k_copy)
    gq_in[me] = gq_out[me]
    st_res[me] = st_fin[me]

    whole(x_in, n_send, n_recv).wait_recv()
    extras = x_in[...].astype(F32)
    later_norms = jnp.sum(
        jnp.where(lax.broadcasted_iota(jnp.int32, extras.shape, 0) > me, extras, 0.0), axis=0
    )
    summed = jnp.sum(jnp.where(extra_row < 8, 0.0, jnp.sum(extras, axis=0)), axis=0, keepdims=True)
    e_out[...] = jnp.broadcast_to(summed * 0.25, e_out.shape)

    def e_copy(p, s):
        return pltpu.make_async_remote_copy(
            src_ref=e_out, dst_ref=e_in.at[s], send_sem=e_send.at[p], recv_sem=e_recv.at[s],
            device_id=(me, p), device_id_type=MESH,
        )

    head_mates(lambda p: e_copy(p, my_head).start())
    for g in range(heads):
        norm = jnp.broadcast_to(later_norms[g : g + 1], (rows, feat2)).T
        ldfk[g] += norm

    whole(st_res, b_send, b_recv).wait_recv()
    for g in order:
        later = jnp.concatenate([st_res[j * heads + g] for j in range(per_head)], axis=0)
        dfk = ldfk[g] + dot(later, v_t)
        dlk = feature_grad(fkp[g], dfk).astype(BF16)
        part = dot(dlk, k_ref[...]).astype(BF16)
        for j in range(grad_per_head):
            gk_out[j * heads + g] = part[j * grad_rows : (j + 1) * grad_rows]
        to_others(range(g, grad_pieces, heads), k_copy)

    def g_copy(d):
        return copy(g_fin, g_res.at[me], g_send, g_recv, d)

    gk_in[me] = gk_out[me]
    whole(gq_in, q_send, q_recv).wait_recv()
    g_fin[:grad_rows] = jnp.sum(gq_in[...].astype(F32), axis=0).astype(BF16)
    whole(gk_in, k_send, k_recv).wait_recv()
    g_fin[grad_rows:] = jnp.sum(gk_in[...].astype(F32), axis=0).astype(BF16)
    peers(lambda d: g_copy(d).start())
    g_res[me] = g_fin[...]

    e_in[my_head] = e_out[...]
    head_mates(lambda s: e_copy(0, s).wait_recv())
    entries = n * rows * heads * heads_axis * hd
    err_ref[...] = jnp.sum(e_in[...], axis=0) / entries
    head_mates(lambda p: e_copy(p, my_head).wait_send())
    x_copy(level).wait_send()
    c_copy(level).wait_send()
    loop(level + 1, levels, lambda up: z_copy(up).wait_send())

    def relay_end(t):
        x_copy(t).wait_send()
        c_copy(t).wait_send()

    loop(0, level, relay_end)
    loop(0, level + 1, lambda t: f_copy(t).wait_send())
    whole(st_in, a_send, a_recv).wait_send()
    whole(st_res, b_send, b_recv).wait_send()
    whole(x_in, n_send, n_recv).wait_send()
    whole(gq_in, q_send, q_recv).wait_send()
    whole(gk_in, k_send, k_recv).wait_send()
    whole(g_res, g_send, g_recv).wait_recv()
    for g in range(heads):
        both = jnp.stack([g_res[j * heads + g] for j in range(grad_per_head)]).astype(F32)
        gq_ref[g] = both[:, :grad_rows].reshape(feat, hd)
        gk_ref[g] = both[:, grad_rows:].reshape(feat, hd)
    whole(g_res, g_send, g_recv).wait_send()


def on_device(queries, keys, values, feat_q, feat_k):
    rows, hd = keys.shape
    heads, _, feat = feat_q.shape
    n = lax.axis_size("ctx")
    heads_axis = lax.axis_size("head")
    feat2 = 2 * feat
    state_pieces = min(n, heads * feat2 // 16)
    grad_pieces = min(n, heads * feat // 16)
    dims = (n, heads_axis, rows, heads, hd, feat, state_pieces, grad_pieces)
    piece = heads * feat2 // state_pieces
    grad_rows = heads * feat // grad_pieces
    levels = n // PLANE
    dma = pltpu.SemaphoreType.DMA
    vmem = pl.BlockSpec(memory_space=pltpu.VMEM)
    student, grad_q, grad_k, error = pl.pallas_call(
        functools.partial(kernel, dims),
        out_shape=(
            jax.ShapeDtypeStruct((rows, heads * hd), BF16),
            jax.ShapeDtypeStruct((heads, feat, hd), F32),
            jax.ShapeDtypeStruct((heads, feat, hd), F32),
            jax.ShapeDtypeStruct((8, hd), F32),
        ),
        in_specs=[vmem] * 5,
        out_specs=(vmem,) * 4,
        scratch_shapes=[
            pltpu.VMEM((heads, hd, rows), F32),
            pltpu.VMEM((heads, 1, rows), F32),
            pltpu.VMEM((16, hd), BF16),
            pltpu.VMEM((n, 16, hd), BF16),
            dma(()),
            dma(()),
            dma(()),
            dma(()),
            pltpu.VMEM((n, 2, rows, hd), BF16),
            pltpu.VMEM((heads * rows, hd), BF16),
            pltpu.VMEM((heads, 1, rows), F32),
            pltpu.VMEM((heads, 1, rows), F32),
            pltpu.VMEM((heads, hd, rows), F32),
            pltpu.VMEM((2 * hd, heads * feat2), F32),
            pltpu.VMEM((heads * feat2, 2 * hd), F32),
            pltpu.VMEM((heads, feat2, rows), F32),
            pltpu.VMEM((heads, feat2, rows), F32),
            pltpu.VMEM((heads, feat2, rows), F32),
            pltpu.VMEM((heads, feat2, rows), F32),
            pltpu.VMEM((n, piece, hd), BF16),
            pltpu.VMEM((n, piece, hd), BF16),
            pltpu.VMEM((n, piece, hd), BF16),
            pltpu.VMEM((n, piece, hd), BF16),
            pltpu.VMEM((n, grad_rows, hd), BF16),
            pltpu.VMEM((n, grad_rows, hd), BF16),
            pltpu.VMEM((n, grad_rows, hd), BF16),
            pltpu.VMEM((n, grad_rows, hd), BF16),
            pltpu.VMEM((2 * grad_rows, hd), BF16),
            pltpu.VMEM((n, 2 * grad_rows, hd), BF16),
            pltpu.VMEM((8, hd), F32),
            pltpu.VMEM((heads_axis, 8, hd), F32),
            dma((levels,)),
            dma((levels,)),
            dma((2, levels)),
            dma((n,)),
            dma(()),
            dma(()),
            dma(()),
            dma(()),
            dma(()),
            dma(()),
            dma(()),
            dma(()),
            dma((heads_axis,)),
            dma((heads_axis,)),
        ],
        compiler_params=pltpu.CompilerParams(
            collective_id=0, has_side_effects=True
        ),
    )(queries, keys, values, feat_q.swapaxes(1, 2), feat_k.swapaxes(1, 2))
    return student, grad_q.swapaxes(1, 2), grad_k.swapaxes(1, 2), error[0, 0]


def solution(mesh):
    in_specs = (
        P("ctx", "head"),
        P("ctx", "head"),
        P("ctx", "head"),
        P("head", None, None),
        P("head", None, None),
    )
    out_specs = (P("ctx", "head"), P("head", None, None), P("head", None, None), P())
    return jax.shard_map(
        on_device, mesh=mesh, in_specs=in_specs, out_specs=out_specs, check_vma=False
    )
```
